32 devices in a mesh: dom: 8 (over z, x), slab: 4 (over y, core).
Axes of the slice: x: 2, y: 2, z: 4, core: 2. Of those that a mesh axis runs over, the one named last changes fastest.
Arguments:
- logperm: float32 [32, 16, 64, 128], P('dom', 'slab'), may hold values from -4.2 to 4.2
- source: float32 [16, 64, 128], P('slab'), may hold values from -6 to 6
- observed: float32 [16, 64, 128], P('slab'), may hold values from -1.2 to 1.2
- brownian: float32 [32, 32], replicated, may hold values from -6 to 6
Outputs:
- particles_next: float32 [32, 16, 64, 128], P('dom', 'slab')
The draws below stay inside these ranges and needn't reach their ends.
All inputs are finite; a program needn't handle non-finite values.
Results may differ from the reference program's by a relative error of at most 0.0003.
Values sent between devices are 32-bit elements; how exact they have to be, the bound alone decides.
A program may use at most 64 MiB of HBM per device.

```python
import math
import jax
import jax.numpy as jnp
from jax import lax

PART_DEV = 4
NY = 64
NZ = 128
SWEEPS = 8
J = 32
NXG = 16
CELLS = 131072


def block_scale(rng, shape, shards, least, high):
    gain = 1.0
    for axis_at, parts in shards:
        heights = jax.random.uniform(jax.random.fold_in(jax.random.fold_in(rng, 6), axis_at), (parts,), jnp.float32, least / len(shards), high / len(shards))
        gain = gain * jnp.repeat(jnp.exp(heights), shape[axis_at] // parts).reshape((-1,) + (1,) * (len(shape) - 1 - axis_at))
    return gain


def normal_values(stream_key, shape, scale, limit, split=(), held_as=jnp.bfloat16):
    array = jax.random.normal(stream_key, shape, jnp.float32) * scale
    if len(split) > 0:
        array = block_scale(stream_key, shape, split, -0.22, 0.18) * array
    return jnp.clip(array, min=-limit, max=limit).astype(held_as)


def setup_inputs(seed: int = 0) -> dict:
    splits = jax.random.split(jax.random.key(seed), 5)
    return {
        "logperm": normal_values(splits[0], (J, NXG, NY, NZ), 0.7, 4.2, ((0, 8), (1, 4)), jnp.float32),
        "source": normal_values(splits[1], (NXG, NY, NZ), 1.0, 6.0, ((0, 4),), jnp.float32),
        "observed": normal_values(splits[2], (NXG, NY, NZ), 0.2, 1.2, ((0, 4),), jnp.float32),
        "brownian": normal_values(splits[3], (J, J), 1.0, 6.0, (), jnp.float32),
    }


misfit_weight = 1000.0

def neighbor_sum(core, below, above, fill):
    pad_y = jnp.pad(core, ((0, 0), (0, 0), (1, 1), (0, 0)), constant_values=fill)
    pad_z = jnp.pad(core, ((0, 0), (0, 0), (0, 0), (1, 1)), constant_values=fill)
    return below + above + pad_y[:, :, :-2] + pad_y[:, :, 2:] + pad_z[..., :-2] + pad_z[..., 2:]

def grad_field(e_core, e_below, e_above, p_core, p_below, p_above, q_core, q_below, q_above):
    summed = e_below * (p_core - p_below) * (q_core - q_below) + e_above * (p_core - p_above) * (q_core - q_above)
    for dimension in (2, 3):
        padding = [(0, 0), (0, 0), (0, 0), (0, 0)]
        padding[dimension] = (1, 1)
        e_pad = jnp.pad(e_core, padding, constant_values=1.0)
        p_pad = jnp.pad(p_core, padding)
        q_pad = jnp.pad(q_core, padding)
        extent = e_core.shape[dimension]
        for offset in (0, 2):
            e_near = lax.slice_in_dim(e_pad, offset, offset + extent, axis=dimension)
            p_near = lax.slice_in_dim(p_pad, offset, offset + extent, axis=dimension)
            q_near = lax.slice_in_dim(q_pad, offset, offset + extent, axis=dimension)
            summed = summed + e_near * (p_core - p_near) * (q_core - q_near)
    return -0.5 * e_core * summed

def field_gradient(block, source, observed):
    e_core = jnp.exp(0.5 * block)
    e_pad = jnp.pad(e_core, ((0, 0), (1, 1), (0, 0), (0, 0)), constant_values=1.0)
    inverse = 1.0 / neighbor_sum(e_core, e_pad[:, :-2], e_pad[:, 2:], 1.0)

    def relax(rhs):
        value = inverse * rhs
        for sweep_index in range(SWEEPS - 1):
            padded = jnp.pad(value, ((0, 0), (1, 1), (0, 0), (0, 0)))
            value = inverse * (rhs + e_core * neighbor_sum(value, padded[:, :-2], padded[:, 2:], 0.0))
        return value / e_core
    pressure = relax(source)
    misfit = misfit_weight * (pressure - observed)
    adjoint = relax(misfit)
    p_pad = jnp.pad(pressure, ((0, 0), (1, 1), (0, 0), (0, 0)))
    q_pad = jnp.pad(adjoint, ((0, 0), (1, 1), (0, 0), (0, 0)))
    return grad_field(e_core, e_pad[:, :-2], e_pad[:, 2:], pressure, p_pad[:, :-2], p_pad[:, 2:], adjoint, q_pad[:, :-2], q_pad[:, 2:])

def reference(logperm, source, observed, brownian):
    blocks = logperm.reshape(J // PART_DEV, PART_DEV, NXG, NY, NZ)

    def per_block(block):
        return field_gradient(block, source[None], observed[None])
    gradient = lax.map(per_block, blocks).reshape(J, CELLS)
    members = logperm.reshape(J, CELLS)
    centre = lax.optimization_barrier(jnp.mean(members, axis=0, keepdims=True))
    spread = members - centre
    gram = jnp.dot(spread, gradient.T, precision=lax.Precision.HIGHEST, preferred_element_type=jnp.float32)
    step_size = J / (4.0 * (CELLS + 1))
    mixing = -(step_size / J) * gram + math.sqrt(2.0 * step_size / J) * brownian
    moved = centre + 1.25 * spread + jnp.dot(mixing.T, spread, precision=lax.Precision.HIGHEST, preferred_element_type=jnp.float32)
    return moved.reshape(logperm.shape)
```

```python
import math

import jax
import jax.numpy as jnp
from jax import lax
from jax.experimental import pallas as pl
from jax.experimental.pallas import tpu as pltpu
from jax.sharding import PartitionSpec as P

SWEEPS = 8
misfit_weight = 1000.0
VMEM_BYTES = 48 * 1024 * 1024
TOP = 8


def lane_masks(shape):
    lane = lax.broadcasted_iota(jnp.int32, shape, len(shape) - 1)
    return lane == 0, lane == shape[-1] - 1


def along_lanes(value, masks, fill):
    depth = value.shape[-1]
    before = jnp.where(masks[0], fill, pltpu.roll(value, 1, value.ndim - 1))
    after = jnp.where(masks[1], fill, pltpu.roll(value, depth - 1, value.ndim - 1))
    return before, after


def neighbors(ref, layer, rows, masks, fill):
    core = ref[layer + 1, TOP : TOP + rows]
    return core, (
        ref[layer, TOP : TOP + rows],
        ref[layer + 2, TOP : TOP + rows],
        ref[layer + 1, TOP - 1 : TOP + rows - 1],
        ref[layer + 1, TOP + 1 : TOP + rows + 1],
        *along_lanes(core, masks, fill),
    )


def border(ref, layers, rows, depth, fill):
    ref[0] = jnp.full((rows + 2 * TOP, depth), fill, jnp.float32)
    ref[layers + 1] = jnp.full((rows + 2 * TOP, depth), fill, jnp.float32)
    edge = jnp.full((layers + 2, TOP, depth), fill, jnp.float32)
    ref[:, 0:TOP] = edge
    ref[:, TOP + rows :] = edge


def scratch_fields(layers, rows, depth):
    padded = pltpu.VMEM((layers + 2, rows + 2 * TOP, depth), jnp.float32)
    plain = pltpu.VMEM((layers, rows, depth), jnp.float32)
    return [padded] * 4 + [plain] * 3


def set_borders(fields, layers, rows, depth):
    border(fields[0], layers, rows, depth, 1.0)
    for ref in fields[1:4]:
        border(ref, layers, rows, depth, 0.0)


def coefficients(logperm, fields):
    e, inverse, gain = fields[0], fields[4], fields[5]
    layers, rows, depth = inverse.shape
    masks = lane_masks((rows, depth))

    def exponent(layer, carry):
        e[layer + 1, TOP : TOP + rows] = jnp.exp(0.5 * logperm(layer))
        return carry

    lax.fori_loop(0, layers, exponent, 0)

    def divide(layer, carry):
        core, near = neighbors(e, layer, rows, masks, 1.0)
        total = 1.0 / (near[0] + near[1] + near[2] + near[3] + near[4] + near[5])
        inverse[layer] = total
        gain[layer] = core * total
        return carry

    lax.fori_loop(0, layers, divide, 0)


def relax(rhs, ping, pong, fields):
    e, inverse, gain, start = fields[0], fields[4], fields[5], fields[6]
    layers, rows, depth = inverse.shape
    masks = lane_masks((rows, depth))

    def first(layer, carry):
        value = inverse[layer] * rhs(layer)
        start[layer] = value
        ping[layer + 1, TOP : TOP + rows] = value
        return carry

    lax.fori_loop(0, layers, first, 0)

    def swept(old, layer):
        _, near = neighbors(old, layer, rows, masks, 0.0)
        total = (near[0] + near[1]) + (near[2] + near[3]) + (near[4] + near[5])
        return start[layer] + gain[layer] * total

    def sweep(old, new):
        def one(layer, carry):
            new[layer + 1, TOP : TOP + rows] = swept(old, layer)
            return carry

        lax.fori_loop(0, layers, one, 0, unroll=2)

    def pair(index, carry):
        sweep(ping, pong)
        sweep(pong, ping)
        return carry

    lax.fori_loop(0, (SWEEPS - 2) // 2, pair, 0)

    def last(layer, carry):
        pong[layer + 1, TOP : TOP + rows] = swept(ping, layer) / e[layer + 1, TOP : TOP + rows]
        return carry

    lax.fori_loop(0, layers, last, 0, unroll=2)


def gradient_layer(layer, fields):
    e, pressure, adjoint = fields[0], fields[2], fields[3]
    _, rows, depth = fields[4].shape
    masks = lane_masks((rows, depth))
    e_core, e_near = neighbors(e, layer, rows, masks, 1.0)
    p_core, p_near = neighbors(pressure, layer, rows, masks, 0.0)
    q_core, q_near = neighbors(adjoint, layer, rows, masks, 0.0)
    total = e_near[0] * (p_core - p_near[0]) * (q_core - q_near[0])
    for side in range(1, 6):
        total = total + e_near[side] * (p_core - p_near[side]) * (q_core - q_near[side])
    return -0.5 * e_core * total


def solve_kernel(logperm, source, observed, gradient, *fields):
    layers, rows, depth = gradient.shape
    set_borders(fields, layers, rows, depth)
    coefficients(lambda layer: logperm[layer], fields)
    relax(lambda layer: source[layer], fields[1], fields[2], fields)
    pressure = fields[2]

    def misfit(layer):
        return misfit_weight * (pressure[layer + 1, TOP : TOP + rows] - observed[layer])

    relax(misfit, fields[1], fields[3], fields)

    def store(layer, carry):
        gradient[layer] = gradient_layer(layer, fields)
        return carry

    lax.fori_loop(0, layers, store, 0)


def solve(logperm, source, observed):
    layers, rows, depth = logperm.shape
    return pl.pallas_call(
        solve_kernel,
        out_shape=jax.ShapeDtypeStruct(logperm.shape, jnp.float32),
        in_specs=[pl.BlockSpec(memory_space=pltpu.VMEM)] * 3,
        out_specs=pl.BlockSpec(memory_space=pltpu.VMEM),
        scratch_shapes=scratch_fields(layers, rows, depth),
        compiler_params=pltpu.CompilerParams(vmem_limit_bytes=VMEM_BYTES),
        cost_estimate=pl.CostEstimate(
            flops=logperm.size * 250, bytes_accessed=logperm.size * 16, transcendentals=logperm.size
        ),
        name="solve",
    )(logperm, source, observed)


def on_device(logperm, source, observed, brownian):
    particles, width, rows, depth = logperm.shape
    slabs, doms = lax.axis_size("slab"), lax.axis_size("dom")
    assert particles == slabs
    layers = width * slabs
    cells = layers * rows * depth
    ensemble = particles * doms
    whole = lax.all_to_all(logperm, "slab", split_axis=0, concat_axis=1, tiled=True)[0]
    full_source = lax.all_gather(source, "slab", axis=0, tiled=True)
    full_observed = lax.all_gather(observed, "slab", axis=0, tiled=True)
    u_cells = lax.all_to_all(
        logperm.reshape(particles, -1), "dom", split_axis=1, concat_axis=0, tiled=True
    )
    centre = jnp.mean(u_cells, axis=0, keepdims=True)
    spread = u_cells - centre
    gradient = solve(whole, full_source, full_observed)
    g_slab = lax.all_to_all(
        gradient.reshape(slabs, 1, -1), "slab", split_axis=0, concat_axis=1, tiled=True
    )[0]
    g_cells = lax.all_to_all(g_slab, "dom", split_axis=1, concat_axis=0, tiled=True)
    partial_gram = lax.dot_general(
        spread,
        g_cells,
        (((1,), (1,)), ((), ())),
        precision=lax.Precision.HIGHEST,
        preferred_element_type=jnp.float32,
    )
    gram = lax.psum(partial_gram, ("dom", "slab"))
    step_size = ensemble / (4.0 * (cells + 1))
    mixing = -(step_size / ensemble) * gram + math.sqrt(2.0 * step_size / ensemble) * brownian
    moved = (
        centre
        + 1.25 * spread
        + lax.dot_general(
            mixing,
            spread,
            (((0,), (0,)), ((), ())),
            precision=lax.Precision.HIGHEST,
            preferred_element_type=jnp.float32,
        )
    )
    returned = lax.all_to_all(moved, "dom", split_axis=0, concat_axis=1, tiled=True)
    return returned.reshape(logperm.shape)


def solution(mesh):
    return jax.shard_map(
        on_device,
        mesh=mesh,
        in_specs=(P("dom", "slab", None, None), P("slab", None, None), P("slab", None, None), P()),
        out_specs=P("dom", "slab", None, None),
        check_vma=False,
    )
```

```python
import math

import jax
import jax.numpy as jnp
from jax import lax
from jax.experimental import pallas as pl
from jax.experimental.pallas import tpu as pltpu
from jax.sharding import PartitionSpec as P

SWEEPS = 8
misfit_weight = 1000.0
VMEM_BYTES = 48 * 1024 * 1024
TOP = 8


def lane_masks(shape):
    lane = lax.broadcasted_iota(jnp.int32, shape, len(shape) - 1)
    return lane == 0, lane == shape[-1] - 1


def along_lanes(value, masks, fill):
    depth = value.shape[-1]
    before = jnp.where(masks[0], fill, pltpu.roll(value, 1, value.ndim - 1))
    after = jnp.where(masks[1], fill, pltpu.roll(value, depth - 1, value.ndim - 1))
    return before, after


def neighbors(ref, layer, rows, masks, fill):
    core = ref[layer + 1, TOP : TOP + rows]
    return core, (
        ref[layer, TOP : TOP + rows],
        ref[layer + 2, TOP : TOP + rows],
        ref[layer + 1, TOP - 1 : TOP + rows - 1],
        ref[layer + 1, TOP + 1 : TOP + rows + 1],
        *along_lanes(core, masks, fill),
    )


def border(ref, layers, rows, depth, fill):
    ref[0] = jnp.full((rows + 2 * TOP, depth), fill, jnp.float32)
    ref[layers + 1] = jnp.full((rows + 2 * TOP, depth), fill, jnp.float32)
    edge = jnp.full((layers + 2, TOP, depth), fill, jnp.float32)
    ref[:, 0:TOP] = edge
    ref[:, TOP + rows :] = edge


def scratch_fields(layers, rows, depth):
    padded = pltpu.VMEM((layers + 2, rows + 2 * TOP, depth), jnp.float32)
    plain = pltpu.VMEM((layers, rows, depth), jnp.float32)
    return [padded] * 4 + [plain] * 3


def set_borders(fields, layers, rows, depth):
    border(fields[0], layers, rows, depth, 1.0)
    for ref in fields[1:4]:
        border(ref, layers, rows, depth, 0.0)


def coefficients(logperm, fields):
    e, inverse, gain = fields[0], fields[4], fields[5]
    layers, rows, depth = inverse.shape
    masks = lane_masks((rows, depth))

    def exponent(layer, carry):
        e[layer + 1, TOP : TOP + rows] = jnp.exp(0.5 * logperm(layer))
        return carry

    lax.fori_loop(0, layers, exponent, 0)

    def divide(layer, carry):
        core, near = neighbors(e, layer, rows, masks, 1.0)
        total = 1.0 / (near[0] + near[1] + near[2] + near[3] + near[4] + near[5])
        inverse[layer] = total
        gain[layer] = core * total
        return carry

    lax.fori_loop(0, layers, divide, 0)


def relax(rhs, ping, pong, fields):
    e, inverse, gain, start = fields[0], fields[4], fields[5], fields[6]
    layers, rows, depth = inverse.shape
    masks = lane_masks((rows, depth))

    def first(layer, carry):
        value = inverse[layer] * rhs(layer)
        start[layer] = value
        ping[layer + 1, TOP : TOP + rows] = value
        return carry

    lax.fori_loop(0, layers, first, 0)

    def swept(old, layer):
        _, near = neighbors(old, layer, rows, masks, 0.0)
        total = (near[0] + near[1]) + (near[2] + near[3]) + (near[4] + near[5])
        return start[layer] + gain[layer] * total

    def sweep(old, new):
        def one(layer, carry):
            new[layer + 1, TOP : TOP + rows] = swept(old, layer)
            return carry

        lax.fori_loop(0, layers, one, 0, unroll=2)

    def pair(index, carry):
        sweep(ping, pong)
        sweep(pong, ping)
        return carry

    lax.fori_loop(0, (SWEEPS - 2) // 2, pair, 0)

    def last(layer, carry):
        pong[layer + 1, TOP : TOP + rows] = swept(ping, layer) / e[layer + 1, TOP : TOP + rows]
        return carry

    lax.fori_loop(0, layers, last, 0, unroll=2)


def gradient_layer(layer, fields):
    e, pressure, adjoint = fields[0], fields[2], fields[3]
    _, rows, depth = fields[4].shape
    masks = lane_masks((rows, depth))
    e_core, e_near = neighbors(e, layer, rows, masks, 1.0)
    p_core, p_near = neighbors(pressure, layer, rows, masks, 0.0)
    q_core, q_near = neighbors(adjoint, layer, rows, masks, 0.0)
    total = e_near[0] * (p_core - p_near[0]) * (q_core - q_near[0])
    for side in range(1, 6):
        total = total + e_near[side] * (p_core - p_near[side]) * (q_core - q_near[side])
    return -0.5 * e_core * total


def fused_kernel(
    logperm, source, observed, brownian, moved_out,
    whole, full_source, full_observed, gradient, members, spread, centre, owned, moved, parts,
    noise, slab_send, slab_recv, side_send, side_recv, member_send, member_recv, own_sem,
    gradient_send, gradient_recv, part_send, part_recv, result_send, result_recv, *fields,
):
    dom, slab = lax.axis_index("dom"), lax.axis_index("slab")
    doms, slabs = lax.axis_size("dom"), lax.axis_size("slab")
    particles, width, rows, depth = logperm.shape
    layers = width * slabs
    team = width
    crew = team * slabs
    ensemble = doms * particles
    place = lax.rem(dom, team)
    base = dom - place
    mine = slab * width + place
    column = place * particles + slab

    def remote(src, dst, send, recv, at_dom, at_slab):
        return pltpu.make_async_remote_copy(
            src_ref=src, dst_ref=dst, send_sem=send, recv_sem=recv,
            device_id=(at_dom, at_slab), device_id_type=pl.DeviceIdType.MESH,
        )

    def crew_device(step):
        layer = lax.rem(mine + step, layers)
        return layer, base + lax.rem(layer, width), layer // width

    barrier = pltpu.get_barrier_semaphore()

    def greet_dom(step, carry):
        pl.semaphore_signal(
            barrier, inc=1, device_id=(lax.rem(dom + step, doms), slab), device_id_type=pl.DeviceIdType.MESH
        )
        return carry

    lax.fori_loop(1, doms, greet_dom, 0)

    def greet_slab(step, carry):
        near = lax.rem(slab + 1 + step // team, slabs)
        pl.semaphore_signal(
            barrier, inc=1, device_id=(base + lax.rem(step, team), near), device_id_type=pl.DeviceIdType.MESH
        )
        return carry

    lax.fori_loop(0, crew - team, greet_slab, 0)
    set_borders(fields, layers, rows, depth)
    noise[...] = brownian[...].T
    pl.semaphore_wait(barrier, doms - 1 + crew - team)

    own_block = pltpu.make_async_copy(logperm.at[slab], whole.at[pl.ds(slab * width, width)], own_sem.at[0])
    own_block.start()

    def slab_copy(step):
        near = lax.rem(slab + step, slabs)
        return remote(
            logperm.at[near], whole.at[pl.ds(slab * width, width)],
            slab_send.at[step - 1], slab_recv.at[step - 1], dom, near,
        )

    order = [2, 1, 3]
    for step in order:
        slab_copy(step).start()

    across = lax.rem(slab + 2, slabs)
    beside = slab + 1 - 2 * lax.rem(slab, 2)
    local = []

    def side_copies(which, block, full):
        def at(owner):
            return full.at[pl.ds(owner * width, width)]

        return [
            remote(block, at(slab), side_send.at[which, 0], side_recv.at[which, 0], dom, across),
            remote(block, at(slab), side_send.at[which, 1], side_recv.at[which, 1], dom, beside),
            remote(at(across), at(across), side_send.at[which, 2], side_recv.at[which, 2], dom, beside),
        ]

    sides = [side_copies(0, source, full_source), side_copies(1, observed, full_observed)]
    for which, (block, full) in enumerate(((source, full_source), (observed, full_observed))):
        copy = pltpu.make_async_copy(block, full.at[pl.ds(slab * width, width)], own_sem.at[1 + which])
        copy.start()
        local.append(copy)
    sides[0][0].start()
    sides[0][1].start()

    def member_copy(step):
        target = lax.rem(dom + step, doms)
        return remote(
            logperm.at[:, lax.rem(target, team)], members.at[pl.ds(dom * particles, particles)],
            member_send.at[step - 1], member_recv.at[step - 1], target, slab,
        )

    def start_member(step, carry):
        member_copy(step).start()
        return carry

    lax.fori_loop(1, doms, start_member, 0)
    own_members = pltpu.make_async_copy(
        logperm.at[:, place], members.at[pl.ds(dom * particles, particles)], own_sem.at[3]
    )
    own_members.start()
    sides[1][0].start()
    sides[1][1].start()

    own_block.wait()
    for step in order:
        slab_copy(step).wait_recv()
    coefficients(lambda layer: whole[layer], fields)
    sides[0][0].wait_recv()
    sides[0][2].start()
    sides[0][1].wait_recv()
    local[0].wait()
    sides[0][2].wait_recv()
    relax(lambda layer: full_source[layer], fields[1], fields[2], fields)
    pressure = fields[2]
    sides[1][0].wait_recv()
    sides[1][2].start()
    sides[1][1].wait_recv()
    local[1].wait()
    sides[1][2].wait_recv()

    def misfit(layer):
        return misfit_weight * (pressure[layer + 1, TOP : TOP + rows] - full_observed[layer])

    relax(misfit, fields[1], fields[3], fields)

    def gradient_copy(step):
        layer, at_dom, at_slab = crew_device(step)
        return remote(
            gradient.at[layer], owned.at[pl.ds(column * rows, rows)],
            gradient_send.at[step - 1], gradient_recv.at[step - 1], at_dom, at_slab,
        )

    def send_gradient(step, carry):
        layer = lax.rem(mine + step, layers)
        gradient[layer] = gradient_layer(layer, fields)
        gradient_copy(step).start()
        return carry

    lax.fori_loop(1, layers, send_gradient, 0)
    owned[pl.ds(column * rows, rows)] = gradient_layer(mine, fields)

    def wait_member(step, carry):
        member_copy(step).wait_recv()
        return carry

    own_members.wait()
    lax.fori_loop(1, doms, wait_member, 0)
    for row in range(rows):
        across_cells = members[:, row]
        mean = jnp.sum(across_cells, axis=0, keepdims=True) * (1.0 / ensemble)
        spread[:, row * depth : (row + 1) * depth] = across_cells - mean
        centre[:, row * depth : (row + 1) * depth] = mean

    def wait_gradient(step, carry):
        gradient_copy(step).wait_recv()
        return carry

    lax.fori_loop(1, crew, wait_gradient, 0)
    gram = jnp.zeros((crew, ensemble), jnp.float32)
    piece = min(16, rows)
    for first in range(0, rows, piece):
        held = [owned[pl.ds(row, crew, stride=rows)] for row in range(first, first + piece)]
        gram = gram + lax.dot_general(
            jnp.concatenate(held, axis=1),
            spread[:, first * depth : (first + piece) * depth],
            (((1,), (1,)), ((), ())),
            precision=lax.Precision.HIGHEST,
            preferred_element_type=jnp.float32,
        )
    parts[mine] = gram

    def part_copy(step):
        _, at_dom, at_slab = crew_device(step)
        return remote(
            parts.at[mine], parts.at[mine], part_send.at[step - 1], part_recv.at[step - 1], at_dom, at_slab
        )

    def start_part(step, carry):
        part_copy(step).start()
        return carry

    def wait_part(step, carry):
        part_copy(step).wait_recv()
        return carry

    lax.fori_loop(1, crew, start_part, 0)
    lax.fori_loop(1, crew, wait_part, 0)
    gram = jnp.sum(parts[...], axis=0)
    step_size = ensemble / (4.0 * (layers * rows * depth + 1))
    first_column = pl.multiple_of(base * particles, 8)
    mixing = -(step_size / ensemble) * gram + math.sqrt(2.0 * step_size / ensemble) * noise[
        pl.ds(first_column, crew)
    ]
    for first in range(0, rows, piece):
        cells = slice(first * depth, (first + piece) * depth)
        result = (
            centre[:, cells]
            + 1.25 * spread[pl.ds(first_column, crew), cells]
            + lax.dot_general(
                mixing, spread[:, cells], (((1,), (0,)), ((), ())),
                precision=lax.Precision.HIGHEST, preferred_element_type=jnp.float32,
            )
        )
        for row in range(piece):
            moved[pl.ds(first + row, crew, stride=rows)] = result[:, row * depth : (row + 1) * depth]

    def result_copy(step):
        to = lax.rem(place + step, team)
        return remote(
            moved_rows(to), moved_out.at[:, pl.ds(place * rows, rows)],
            result_send.at[step - 1], result_recv.at[step - 1], base + to, slab,
        )

    def moved_rows(to):
        return moved.reshape(crew, rows, depth).at[pl.ds(to * particles, particles)]

    for step in range(1, team):
        result_copy(step).start()
    own_result = pltpu.make_async_copy(
        moved_rows(place), moved_out.at[:, pl.ds(place * rows, rows)], own_sem.at[4]
    )
    own_result.start()

    for step in order:
        slab_copy(step).wait_send()
    for which in range(2):
        for copy in sides[which]:
            copy.wait_send()

    def sent_member(step, carry):
        member_copy(step).wait_send()
        return carry

    def sent_crew(step, carry):
        gradient_copy(step).wait_send()
        part_copy(step).wait_send()
        return carry

    lax.fori_loop(1, doms, sent_member, 0)
    lax.fori_loop(1, crew, sent_crew, 0)
    own_result.wait()
    for step in range(1, team):
        result_copy(step).wait()


def on_device(logperm, source, observed, brownian):
    particles, width, rows, depth = logperm.shape
    slabs, doms = lax.axis_size("slab"), lax.axis_size("dom")
    assert particles == slabs == 4 and doms % width == 0
    layers, crew, ensemble = width * slabs, width * slabs, doms * particles
    f32 = jnp.float32
    dma = pltpu.SemaphoreType.DMA
    scratch = [
        pltpu.VMEM((layers, rows, depth), f32),
        pltpu.VMEM((layers, rows, depth), f32),
        pltpu.VMEM((layers, rows, depth), f32),
        pltpu.VMEM((layers, rows, depth), f32),
        pltpu.VMEM((ensemble, rows, depth), f32),
        pltpu.VMEM((ensemble, rows * depth), f32),
        pltpu.VMEM((1, rows * depth), f32),
        pltpu.VMEM((crew * rows, depth), f32),
        pltpu.VMEM((crew * rows, depth), f32),
        pltpu.VMEM((crew, crew, ensemble), f32),
        pltpu.VMEM((ensemble, ensemble), f32),
        dma((slabs - 1,)), dma((slabs - 1,)),
        dma((2, 3)), dma((2, 3)),
        dma((doms - 1,)), dma((doms - 1,)),
        dma((5,)),
        dma((crew - 1,)), dma((crew - 1,)),
        dma((crew - 1,)), dma((crew - 1,)),
        dma((width - 1,)), dma((width - 1,)),
        *scratch_fields(layers, rows, depth),
    ]
    anywhere = pl.BlockSpec(memory_space=pl.ANY)
    moved = pl.pallas_call(
        fused_kernel,
        out_shape=jax.ShapeDtypeStruct((particles, width * rows, depth), f32),
        in_specs=[anywhere] * 3 + [pl.BlockSpec(memory_space=pltpu.VMEM)],
        out_specs=anywhere,
        scratch_shapes=scratch,
        compiler_params=pltpu.CompilerParams(
            collective_id=0, has_side_effects=True, vmem_limit_bytes=VMEM_BYTES
        ),
        cost_estimate=pl.CostEstimate(
            flops=logperm.size * 300, bytes_accessed=logperm.size * 16, transcendentals=logperm.size
        ),
        name="langevin",
    )(logperm, source, observed, brownian)
    return moved.reshape(logperm.shape)


def solution(mesh):
    return jax.shard_map(
        on_device,
        mesh=mesh,
        in_specs=(P("dom", "slab", None, None), P("slab", None, None), P("slab", None, None), P()),
        out_specs=P("dom", "slab", None, None),
        check_vma=False,
    )
```

```python
import math

import jax
import jax.numpy as jnp
from jax import lax
from jax.experimental import pallas as pl
from jax.experimental.pallas import tpu as pltpu
from jax.sharding import PartitionSpec as P

SWEEPS = 8
misfit_weight = 1000.0
VMEM_BYTES = 64 * 1024 * 1024 - 128 * 1024
TOP = 8


def lane_masks(shape):
    lane = lax.broadcasted_iota(jnp.int32, shape, len(shape) - 1)
    return lane == 0, lane == shape[-1] - 1


def along_lanes(value, masks, fill):
    depth = value.shape[-1]
    before = jnp.where(masks[0], fill, pltpu.roll(value, 1, value.ndim - 1))
    after = jnp.where(masks[1], fill, pltpu.roll(value, depth - 1, value.ndim - 1))
    return before, after


def neighbors(ref, layer, rows, masks, fill):
    core = ref[layer + 1, TOP : TOP + rows]
    return core, (
        ref[layer, TOP : TOP + rows],
        ref[layer + 2, TOP : TOP + rows],
        ref[layer + 1, TOP - 1 : TOP + rows - 1],
        ref[layer + 1, TOP + 1 : TOP + rows + 1],
        *along_lanes(core, masks, fill),
    )


def border(ref, layers, rows, depth, fill):
    ref[0] = jnp.full((rows + 2 * TOP, depth), fill, jnp.float32)
    ref[layers + 1] = jnp.full((rows + 2 * TOP, depth), fill, jnp.float32)
    edge = jnp.full((layers + 2, TOP, depth), fill, jnp.float32)
    ref[:, 0:TOP] = edge
    ref[:, TOP + rows :] = edge


def scratch_fields(layers, rows, depth):
    padded = pltpu.VMEM((layers + 2, rows + 2 * TOP, depth), jnp.float32)
    plain = pltpu.VMEM((layers, rows, depth), jnp.float32)
    return [padded] * 4 + [plain] * 3


def set_borders(fields, layers, rows, depth):
    border(fields[0], layers, rows, depth, 1.0)
    for ref in fields[1:4]:
        border(ref, layers, rows, depth, 0.0)


def coefficients(logperm, fields):
    e, inverse, gain = fields[0], fields[4], fields[5]
    layers, rows, depth = inverse.shape
    masks = lane_masks((rows, depth))

    def exponent(layer, carry):
        e[layer + 1, TOP : TOP + rows] = jnp.exp(0.5 * logperm(layer))
        return carry

    lax.fori_loop(0, layers, exponent, 0, unroll=8)

    def divide(layer, carry):
        core, near = neighbors(e, layer, rows, masks, 1.0)
        total = 1.0 / (near[0] + near[1] + near[2] + near[3] + near[4] + near[5])
        inverse[layer] = total
        gain[layer] = core * total
        return carry

    lax.fori_loop(0, layers, divide, 0, unroll=8)


def relax(rhs, ping, pong, fields):
    e, inverse, gain, start = fields[0], fields[4], fields[5], fields[6]
    layers, rows, depth = inverse.shape
    masks = lane_masks((rows, depth))

    def first(layer, carry):
        value = inverse[layer] * rhs(layer)
        start[layer] = value
        ping[layer + 1, TOP : TOP + rows] = value
        return carry

    lax.fori_loop(0, layers, first, 0, unroll=8)

    def swept(old, layer):
        _, near = neighbors(old, layer, rows, masks, 0.0)
        total = (near[0] + near[1]) + (near[2] + near[3]) + (near[4] + near[5])
        return start[layer] + gain[layer] * total

    def sweep(old, new):
        def one(layer, carry):
            new[layer + 1, TOP : TOP + rows] = swept(old, layer)
            return carry

        lax.fori_loop(0, layers, one, 0, unroll=layers)

    def pair(index, carry):
        sweep(ping, pong)
        sweep(pong, ping)
        return carry

    lax.fori_loop(0, (SWEEPS - 2) // 2, pair, 0)

    def last(layer, carry):
        pong[layer + 1, TOP : TOP + rows] = swept(ping, layer) / e[layer + 1, TOP : TOP + rows]
        return carry

    lax.fori_loop(0, layers, last, 0, unroll=layers)


def gradient_layer(layer, fields):
    e, pressure, adjoint = fields[0], fields[2], fields[3]
    _, rows, depth = fields[4].shape
    masks = lane_masks((rows, depth))
    e_core, e_near = neighbors(e, layer, rows, masks, 1.0)
    p_core, p_near = neighbors(pressure, layer, rows, masks, 0.0)
    q_core, q_near = neighbors(adjoint, layer, rows, masks, 0.0)
    total = e_near[0] * (p_core - p_near[0]) * (q_core - q_near[0])
    for side in range(1, 6):
        total = total + e_near[side] * (p_core - p_near[side]) * (q_core - q_near[side])
    return -0.5 * e_core * total


def fused_kernel(
    logperm, source, observed, brownian_far, moved_out,
    brownian, whole, full_source, full_observed, gradient, members, spread, centre, owned, moved, parts,
    noise, slab_send, slab_recv, side_send, side_recv, member_send, member_recv, own_sem,
    gradient_send, gradient_recv, part_send, part_recv, result_send, result_recv, *fields,
):
    dom, slab = lax.axis_index("dom"), lax.axis_index("slab")
    doms, slabs = lax.axis_size("dom"), lax.axis_size("slab")
    particles, width, rows, depth = logperm.shape
    layers = width * slabs
    team = width
    crew = team * slabs
    ensemble = doms * particles
    place = lax.rem(dom, team)
    base = dom - place
    mine = slab * width + place
    column = place * particles + slab

    def remote(src, dst, send, recv, at_dom, at_slab):
        return pltpu.make_async_remote_copy(
            src_ref=src, dst_ref=dst, send_sem=send, recv_sem=recv,
            device_id=(at_dom, at_slab), device_id_type=pl.DeviceIdType.MESH,
        )

    def crew_device(step):
        layer = lax.rem(mine + step, layers)
        return layer, base + lax.rem(layer, width), layer // width

    fetch = pltpu.make_async_copy(brownian_far, brownian, own_sem.at[5])
    fetch.start()
    barrier = pltpu.get_barrier_semaphore()

    def greet_dom(step, carry):
        pl.semaphore_signal(
            barrier, inc=1, device_id=(lax.rem(dom + step, doms), slab), device_id_type=pl.DeviceIdType.MESH
        )
        return carry

    lax.fori_loop(1, doms, greet_dom, 0)

    def greet_slab(step, carry):
        near = lax.rem(slab + 1 + step // team, slabs)
        pl.semaphore_signal(
            barrier, inc=1, device_id=(base + lax.rem(step, team), near), device_id_type=pl.DeviceIdType.MESH
        )
        return carry

    lax.fori_loop(0, crew - team, greet_slab, 0)
    set_borders(fields, layers, rows, depth)
    pl.semaphore_wait(barrier, doms - 1 + crew - team)

    own_block = pltpu.make_async_copy(logperm.at[slab], whole.at[pl.ds(slab * width, width)], own_sem.at[0])
    own_block.start()

    def slab_copy(step):
        near = lax.rem(slab + step, slabs)
        return remote(
            logperm.at[near], whole.at[pl.ds(slab * width, width)],
            slab_send.at[step - 1], slab_recv.at[step - 1], dom, near,
        )

    order = [2, 1, 3]
    for step in order:
        slab_copy(step).start()

    across = lax.rem(slab + 2, slabs)
    beside = slab + 1 - 2 * lax.rem(slab, 2)
    local = []

    def side_copies(which, block, full):
        def at(owner):
            return full.at[pl.ds(owner * width, width)]

        return [
            remote(block, at(slab), side_send.at[which, 0], side_recv.at[which, 0], dom, across),
            remote(block, at(slab), side_send.at[which, 1], side_recv.at[which, 1], dom, beside),
            remote(at(across), at(across), side_send.at[which, 2], side_recv.at[which, 2], dom, beside),
        ]

    sides = [side_copies(0, source, full_source), side_copies(1, observed, full_observed)]
    for which, (block, full) in enumerate(((source, full_source), (observed, full_observed))):
        copy = pltpu.make_async_copy(block, full.at[pl.ds(slab * width, width)], own_sem.at[1 + which])
        copy.start()
        local.append(copy)
    sides[0][0].start()
    sides[0][1].start()

    def member_copy(step):
        target = lax.rem(dom + step, doms)
        return remote(
            logperm.at[:, lax.rem(target, team)], members.at[pl.ds(dom * particles, particles)],
            member_send.at[step - 1], member_recv.at[step - 1], target, slab,
        )

    def start_member(step, carry):
        member_copy(step).start()
        return carry

    lax.fori_loop(1, doms, start_member, 0)
    own_members = pltpu.make_async_copy(
        logperm.at[:, place], members.at[pl.ds(dom * particles, particles)], own_sem.at[3]
    )
    own_members.start()

    fetch.wait()
    noise[...] = brownian[...].T
    own_block.wait()
    for step in order:
        slab_copy(step).wait_recv()
    sides[1][0].start()
    sides[1][1].start()
    coefficients(lambda layer: whole[layer], fields)
    sides[0][0].wait_recv()
    sides[0][2].start()
    sides[0][1].wait_recv()
    local[0].wait()
    sides[0][2].wait_recv()
    relax(lambda layer: full_source[layer], fields[1], fields[2], fields)
    pressure = fields[2]
    sides[1][0].wait_recv()
    sides[1][2].start()
    sides[1][1].wait_recv()
    local[1].wait()
    sides[1][2].wait_recv()

    def misfit(layer):
        return misfit_weight * (pressure[layer + 1, TOP : TOP + rows] - full_observed[layer])

    relax(misfit, fields[1], fields[3], fields)

    def gradient_copy(step):
        layer, at_dom, at_slab = crew_device(step)
        return remote(
            gradient.at[layer], owned.at[pl.ds(column * rows, rows)],
            gradient_send.at[step - 1], gradient_recv.at[step - 1], at_dom, at_slab,
        )

    def send_gradient(step, carry):
        layer = lax.rem(mine + step, layers)
        gradient[layer] = gradient_layer(layer, fields)
        gradient_copy(step).start()
        return carry

    lax.fori_loop(1, layers, send_gradient, 0, unroll=3)
    owned[pl.ds(column * rows, rows)] = gradient_layer(mine, fields)

    def wait_member(step, carry):
        member_copy(step).wait_recv()
        return carry

    own_members.wait()
    lax.fori_loop(1, doms, wait_member, 0)
    member_rows = members.reshape(ensemble * rows, depth)
    for row in range(rows):
        across_cells = member_rows[pl.ds(row, ensemble, stride=rows)]
        mean = jnp.sum(across_cells, axis=0, keepdims=True) * (1.0 / ensemble)
        spread[:, row * depth : (row + 1) * depth] = across_cells - mean
        centre[:, row * depth : (row + 1) * depth] = mean

    def wait_gradient(step, carry):
        gradient_copy(step).wait_recv()
        return carry

    lax.fori_loop(1, crew, wait_gradient, 0)
    gram = jnp.zeros((crew, ensemble), jnp.float32)
    piece = min(16, rows)
    for first in range(0, rows, piece):
        held = [owned[pl.ds(row, crew, stride=rows)] for row in range(first, first + piece)]
        gram = gram + lax.dot_general(
            jnp.concatenate(held, axis=1),
            spread[:, first * depth : (first + piece) * depth],
            (((1,), (1,)), ((), ())),
            precision=lax.Precision.HIGHEST,
            preferred_element_type=jnp.float32,
        )
    parts[mine] = gram

    def part_copy(step):
        _, at_dom, at_slab = crew_device(step)
        return remote(
            parts.at[mine], parts.at[mine], part_send.at[step - 1], part_recv.at[step - 1], at_dom, at_slab
        )

    def start_part(step, carry):
        part_copy(step).start()
        return carry

    def wait_part(step, carry):
        part_copy(step).wait_recv()
        return carry

    lax.fori_loop(1, crew, start_part, 0)
    lax.fori_loop(1, crew, wait_part, 0)
    gram = jnp.sum(parts[...], axis=0)
    step_size = ensemble / (4.0 * (layers * rows * depth + 1))
    first_column = pl.multiple_of(base * particles, 8)
    mixing = -(step_size / ensemble) * gram + math.sqrt(2.0 * step_size / ensemble) * noise[
        pl.ds(first_column, crew)
    ]
    for first in range(0, rows, piece):
        cells = slice(first * depth, (first + piece) * depth)
        result = (
            centre[:, cells]
            + 1.25 * spread[pl.ds(first_column, crew), cells]
            + lax.dot_general(
                mixing, spread[:, cells], (((1,), (0,)), ((), ())),
                precision=lax.Precision.HIGHEST, preferred_element_type=jnp.float32,
            )
        )
        for row in range(piece):
            moved[pl.ds(first + row, crew, stride=rows)] = result[:, row * depth : (row + 1) * depth]

    def result_copy(step):
        to = lax.rem(place + step, team)
        return remote(
            moved_rows(to), moved_out.at[:, pl.ds(place * rows, rows)],
            result_send.at[step - 1], result_recv.at[step - 1], base + to, slab,
        )

    def moved_rows(to):
        return moved.reshape(crew, rows, depth).at[pl.ds(to * particles, particles)]

    for step in range(1, team):
        result_copy(step).start()
    own_result = pltpu.make_async_copy(
        moved_rows(place), moved_out.at[:, pl.ds(place * rows, rows)], own_sem.at[4]
    )
    own_result.start()

    for step in order:
        slab_copy(step).wait_send()
    for which in range(2):
        for copy in sides[which]:
            copy.wait_send()

    def sent_member(step, carry):
        member_copy(step).wait_send()
        return carry

    def sent_crew(step, carry):
        gradient_copy(step).wait_send()
        part_copy(step).wait_send()
        return carry

    lax.fori_loop(1, doms, sent_member, 0)
    lax.fori_loop(1, crew, sent_crew, 0)
    own_result.wait()
    for step in range(1, team):
        result_copy(step).wait()


def on_device(logperm, source, observed, brownian):
    particles, width, rows, depth = logperm.shape
    slabs, doms = lax.axis_size("slab"), lax.axis_size("dom")
    assert particles == slabs == 4 and doms % width == 0
    layers, crew, ensemble = width * slabs, width * slabs, doms * particles
    f32 = jnp.float32
    dma = pltpu.SemaphoreType.DMA
    scratch = [
        pltpu.VMEM((ensemble, ensemble), f32),
        pltpu.VMEM((layers, rows, depth), f32),
        pltpu.VMEM((layers, rows, depth), f32),
        pltpu.VMEM((layers, rows, depth), f32),
        pltpu.VMEM((layers, rows, depth), f32),
        pltpu.VMEM((ensemble, rows, depth), f32),
        pltpu.VMEM((ensemble, rows * depth), f32),
        pltpu.VMEM((1, rows * depth), f32),
        pltpu.VMEM((crew * rows, depth), f32),
        pltpu.VMEM((crew * rows, depth), f32),
        pltpu.VMEM((crew, crew, ensemble), f32),
        pltpu.VMEM((ensemble, ensemble), f32),
        dma((slabs - 1,)), dma((slabs - 1,)),
        dma((2, 3)), dma((2, 3)),
        dma((doms - 1,)), dma((doms - 1,)),
        dma((6,)),
        dma((crew - 1,)), dma((crew - 1,)),
        dma((crew - 1,)), dma((crew - 1,)),
        dma((width - 1,)), dma((width - 1,)),
        *scratch_fields(layers, rows, depth),
    ]
    far = pl.BlockSpec(memory_space=pltpu.HBM)
    moved = pl.pallas_call(
        fused_kernel,
        out_shape=jax.ShapeDtypeStruct((particles, width * rows, depth), f32),
        in_specs=[far] * 4,
        out_specs=far,
        scratch_shapes=scratch,
        compiler_params=pltpu.CompilerParams(
            collective_id=0, has_side_effects=True, vmem_limit_bytes=VMEM_BYTES
        ),
        cost_estimate=pl.CostEstimate(
            flops=logperm.size * 300, bytes_accessed=logperm.size * 16, transcendentals=logperm.size
        ),
        name="langevin",
    )(logperm, source, observed, brownian)
    return moved.reshape(logperm.shape)


def solution(mesh):
    return jax.shard_map(
        on_device,
        mesh=mesh,
        in_specs=(P("dom", "slab", None, None), P("slab", None, None), P("slab", None, None), P()),
        out_specs=P("dom", "slab", None, None),
        check_vma=False,
    )
```

```python
import math

import jax
import jax.numpy as jnp
from jax import lax
from jax.experimental import pallas as pl
from jax.experimental.pallas import tpu as pltpu
from jax.sharding import PartitionSpec as P

SWEEPS = 8
misfit_weight = 1000.0
VMEM_BYTES = 64 * 1024 * 1024 - 128 * 1024
SUB = 8


def interleaved(ref, layer, rows):
    step = rows // SUB
    first = layer * rows
    return jnp.concatenate([ref[pl.ds(first + v, SUB, stride=step)] for v in range(step)], axis=0)


def edge_masks(depth):
    lane = lax.broadcasted_iota(jnp.int32, (SUB, depth), 1)
    sublane = lax.broadcasted_iota(jnp.int32, (SUB, depth), 0)
    return lane == 0, lane == depth - 1, sublane == 0, sublane == SUB - 1


def neighbors(ref, layer, masks, fill):
    core = ref[layer + 1]
    rows, depth = core.shape
    tiles = [core[at : at + SUB] for at in range(0, rows, SUB)]
    before = [jnp.where(masks[2], fill, pltpu.roll(tiles[-1], 1, 0))] + tiles[:-1]
    after = tiles[1:] + [jnp.where(masks[3], fill, pltpu.roll(tiles[0], SUB - 1, 0))]
    left = [jnp.where(masks[0], fill, pltpu.roll(tile, 1, 1)) for tile in tiles]
    right = [jnp.where(masks[1], fill, pltpu.roll(tile, depth - 1, 1)) for tile in tiles]
    joined = [jnp.concatenate(side, axis=0) for side in (before, after, left, right)]
    return core, (ref[layer], ref[layer + 2], *joined)


def border(ref, layers, rows, depth, fill):
    ref[0] = jnp.full((rows, depth), fill, jnp.float32)
    ref[layers + 1] = jnp.full((rows, depth), fill, jnp.float32)


def scratch_fields(layers, rows, depth):
    padded = pltpu.VMEM((layers + 2, rows, depth), jnp.float32)
    plain = pltpu.VMEM((layers, rows, depth), jnp.float32)
    return [padded] * 4 + [plain] * 3


def set_borders(fields, layers, rows, depth):
    border(fields[0], layers, rows, depth, 1.0)
    for ref in fields[1:4]:
        border(ref, layers, rows, depth, 0.0)


def coefficients(logperm, fields):
    e, inverse, gain = fields[0], fields[4], fields[5]
    layers, rows, depth = inverse.shape
    masks = edge_masks(depth)

    def exponent(layer, carry):
        e[layer + 1] = jnp.exp(0.5 * logperm(layer))
        return carry

    lax.fori_loop(0, layers, exponent, 0, unroll=8)

    def divide(layer, carry):
        core, near = neighbors(e, layer, masks, 1.0)
        total = 1.0 / (near[0] + near[1] + near[2] + near[3] + near[4] + near[5])
        inverse[layer] = total
        gain[layer] = core * total
        return carry

    lax.fori_loop(0, layers, divide, 0, unroll=8)


def relax(rhs, ping, pong, fields):
    e, inverse, gain, start = fields[0], fields[4], fields[5], fields[6]
    layers, rows, depth = inverse.shape
    masks = edge_masks(depth)

    def first(layer, carry):
        value = inverse[layer] * rhs(layer)
        start[layer] = value
        ping[layer + 1] = value
        return carry

    lax.fori_loop(0, layers, first, 0, unroll=8)

    def swept(old, layer):
        _, near = neighbors(old, layer, masks, 0.0)
        total = (near[0] + near[1]) + (near[2] + near[3]) + (near[4] + near[5])
        return start[layer] + gain[layer] * total

    def sweep(old, new):
        def one(layer, carry):
            new[layer + 1] = swept(old, layer)
            return carry

        lax.fori_loop(0, layers, one, 0, unroll=layers)

    def pair(index, carry):
        sweep(ping, pong)
        sweep(pong, ping)
        return carry

    lax.fori_loop(0, (SWEEPS - 2) // 2, pair, 0)

    def last(layer, carry):
        pong[layer + 1] = swept(ping, layer) / e[layer + 1]
        return carry

    lax.fori_loop(0, layers, last, 0, unroll=layers)


def gradient_layer(layer, fields):
    e, pressure, adjoint = fields[0], fields[2], fields[3]
    _, rows, depth = fields[4].shape
    masks = edge_masks(depth)
    e_core, e_near = neighbors(e, layer, masks, 1.0)
    p_core, p_near = neighbors(pressure, layer, masks, 0.0)
    q_core, q_near = neighbors(adjoint, layer, masks, 0.0)
    total = e_near[0] * (p_core - p_near[0]) * (q_core - q_near[0])
    for side in range(1, 6):
        total = total + e_near[side] * (p_core - p_near[side]) * (q_core - q_near[side])
    return -0.5 * e_core * total


def fused_kernel(
    logperm, source, observed, brownian_far, moved_out,
    brownian, whole, full_source, full_observed, gradient, members, spread, centre, owned, moved, parts,
    noise, slab_send, slab_recv, side_send, side_recv, member_send, member_recv, own_sem,
    gradient_send, gradient_recv, part_send, part_recv, result_send, result_recv, *fields,
):
    dom, slab = lax.axis_index("dom"), lax.axis_index("slab")
    doms, slabs = lax.axis_size("dom"), lax.axis_size("slab")
    particles, width, rows, depth = logperm.shape
    layers = width * slabs
    team = width
    crew = team * slabs
    ensemble = doms * particles
    place = lax.rem(dom, team)
    base = dom - place
    mine = slab * width + place
    column = place * particles + slab

    def remote(src, dst, send, recv, at_dom, at_slab):
        return pltpu.make_async_remote_copy(
            src_ref=src, dst_ref=dst, send_sem=send, recv_sem=recv,
            device_id=(at_dom, at_slab), device_id_type=pl.DeviceIdType.MESH,
        )

    def crew_device(step):
        layer = lax.rem(mine + step, layers)
        return layer, base + lax.rem(layer, width), layer // width

    fetch = pltpu.make_async_copy(brownian_far, brownian, own_sem.at[5])
    fetch.start()
    barrier = pltpu.get_barrier_semaphore()

    def greet_dom(step, carry):
        pl.semaphore_signal(
            barrier, inc=1, device_id=(lax.rem(dom + step, doms), slab), device_id_type=pl.DeviceIdType.MESH
        )
        return carry

    lax.fori_loop(1, doms, greet_dom, 0)

    def greet_slab(step, carry):
        near = lax.rem(slab + 1 + step // team, slabs)
        pl.semaphore_signal(
            barrier, inc=1, device_id=(base + lax.rem(step, team), near), device_id_type=pl.DeviceIdType.MESH
        )
        return carry

    lax.fori_loop(0, crew - team, greet_slab, 0)
    set_borders(fields, layers, rows, depth)
    pl.semaphore_wait(barrier, doms - 1 + crew - team)

    whole_blocks = whole.reshape(layers, rows, depth)
    own_block = pltpu.make_async_copy(logperm.at[slab], whole_blocks.at[pl.ds(slab * width, width)], own_sem.at[0])
    own_block.start()

    def slab_copy(step):
        near = lax.rem(slab + step, slabs)
        return remote(
            logperm.at[near], whole_blocks.at[pl.ds(slab * width, width)],
            slab_send.at[step - 1], slab_recv.at[step - 1], dom, near,
        )

    order = [2, 1, 3]
    for step in order:
        slab_copy(step).start()

    across = lax.rem(slab + 2, slabs)
    beside = slab + 1 - 2 * lax.rem(slab, 2)
    local = []

    def side_copies(which, block, full):
        def at(owner):
            return full.reshape(layers, rows, depth).at[pl.ds(owner * width, width)]

        return [
            remote(block, at(slab), side_send.at[which, 0], side_recv.at[which, 0], dom, across),
            remote(block, at(slab), side_send.at[which, 1], side_recv.at[which, 1], dom, beside),
            remote(at(across), at(across), side_send.at[which, 2], side_recv.at[which, 2], dom, beside),
        ]

    sides = [side_copies(0, source, full_source), side_copies(1, observed, full_observed)]
    for which, (block, full) in enumerate(((source, full_source), (observed, full_observed))):
        copy = pltpu.make_async_copy(block, full.reshape(layers, rows, depth).at[pl.ds(slab * width, width)], own_sem.at[1 + which])
        copy.start()
        local.append(copy)
    sides[0][0].start()
    sides[0][1].start()

    def member_copy(step):
        target = lax.rem(base + team * (1 + step // team), doms) + lax.rem(place + step, team)
        return remote(
            logperm.at[:, lax.rem(target, team)], members.at[pl.ds(dom * particles, particles)],
            member_send.at[step], member_recv.at[step], target, slab,
        )

    def each_member(act):
        def body(step, carry):
            act(member_copy(step))
            return carry

        lax.fori_loop(0, doms - team, body, 0)
        lax.fori_loop(doms - team + 1, doms, body, 0)

    each_member(lambda copy: copy.start())
    own_members = pltpu.make_async_copy(
        logperm.at[:, place], members.at[pl.ds(dom * particles, particles)], own_sem.at[3]
    )
    own_members.start()

    fetch.wait()
    noise[...] = brownian[...].T
    own_block.wait()
    for step in order:
        slab_copy(step).wait_recv()
    sides[1][0].start()
    sides[1][1].start()
    coefficients(lambda layer: interleaved(whole, layer, rows), fields)
    sides[0][0].wait_recv()
    sides[0][2].start()
    sides[0][1].wait_recv()
    local[0].wait()
    sides[0][2].wait_recv()
    relax(lambda layer: interleaved(full_source, layer, rows), fields[1], fields[2], fields)
    pressure = fields[2]
    sides[1][0].wait_recv()
    sides[1][2].start()
    sides[1][1].wait_recv()
    local[1].wait()
    sides[1][2].wait_recv()

    def misfit(layer):
        return misfit_weight * (pressure[layer + 1] - interleaved(full_observed, layer, rows))

    relax(misfit, fields[1], fields[3], fields)

    def gradient_copy(step):
        layer, at_dom, at_slab = crew_device(step)
        return remote(
            gradient.at[layer], owned.at[pl.ds(column * rows, rows)],
            gradient_send.at[step - 1], gradient_recv.at[step - 1], at_dom, at_slab,
        )

    def send_gradient(step, carry):
        layer = lax.rem(mine + step, layers)
        gradient[layer] = gradient_layer(layer, fields)
        gradient_copy(step).start()
        return carry

    lax.fori_loop(1, layers, send_gradient, 0, unroll=5)
    owned[pl.ds(column * rows, rows)] = gradient_layer(mine, fields)

    own_members.wait()
    each_member(lambda copy: copy.wait_recv())
    member_rows = members.reshape(ensemble * rows, depth)
    for row in range(rows):
        across_cells = member_rows[pl.ds(row, ensemble, stride=rows)]
        mean = jnp.sum(across_cells, axis=0, keepdims=True) * (1.0 / ensemble)
        spread[:, row * depth : (row + 1) * depth] = across_cells - mean
        centre[:, row * depth : (row + 1) * depth] = mean

    def wait_gradient(step, carry):
        gradient_copy(step).wait_recv()
        return carry

    lax.fori_loop(1, crew, wait_gradient, 0)
    gram = jnp.zeros((crew, ensemble), jnp.float32)
    piece = min(16, rows)
    tiles = rows // SUB
    for first in range(0, rows, piece):
        held = [
            owned[pl.ds(row % tiles * SUB + row // tiles, crew, stride=rows)]
            for row in range(first, first + piece)
        ]
        gram = gram + lax.dot_general(
            jnp.concatenate(held, axis=1),
            spread[:, first * depth : (first + piece) * depth],
            (((1,), (1,)), ((), ())),
            precision=lax.Precision.HIGHEST,
            preferred_element_type=jnp.float32,
        )
    parts[mine] = gram

    def part_copy(step):
        _, at_dom, at_slab = crew_device(step)
        return remote(
            parts.at[mine], parts.at[mine], part_send.at[step - 1], part_recv.at[step - 1], at_dom, at_slab
        )

    def start_part(step, carry):
        part_copy(step).start()
        return carry

    def wait_part(step, carry):
        part_copy(step).wait_recv()
        return carry

    lax.fori_loop(1, crew, start_part, 0)
    lax.fori_loop(1, crew, wait_part, 0)
    gram = jnp.sum(parts[...], axis=0)
    step_size = ensemble / (4.0 * (layers * rows * depth + 1))
    first_column = pl.multiple_of(base * particles, 8)
    mixing = -(step_size / ensemble) * gram + math.sqrt(2.0 * step_size / ensemble) * noise[
        pl.ds(first_column, crew)
    ]
    moved_block = moved.reshape(crew, rows, depth)

    def result_part(to, first):
        return (
            moved_block.at[pl.ds(to * particles, particles), pl.ds(first, part)],
            moved_out.at[:, pl.ds(place * rows + first, part)],
        )

    def result_copy(step, first):
        to = lax.rem(place + step, team)
        at = first // part
        return remote(
            *result_part(to, first), result_send.at[at, step - 1], result_recv.at[at, step - 1],
            base + to, slab,
        )

    part = rows // 2
    own_results = []
    for first in range(0, rows, part):
        cells = slice(first * depth, (first + part) * depth)
        result = lax.dot_general(
            mixing, spread[:, cells], (((1,), (0,)), ((), ())),
            precision=lax.Precision.HIGHEST, preferred_element_type=jnp.float32,
        ) - 0.25 * centre[:, cells]
        for row in range(part):
            moved[pl.ds(first + row, crew, stride=rows)] = result[:, row * depth : (row + 1) * depth]
        for step in range(1, team):
            result_copy(step, first).start()
        copy = pltpu.make_async_copy(*result_part(place, first), own_sem.at[6 + first // part])
        copy.start()
        own_results.append(copy)

    for step in order:
        slab_copy(step).wait_send()
    for which in range(2):
        for copy in sides[which]:
            copy.wait_send()

    def sent_crew(step, carry):
        gradient_copy(step).wait_send()
        part_copy(step).wait_send()
        return carry

    each_member(lambda copy: copy.wait_send())
    lax.fori_loop(1, crew, sent_crew, 0)
    for copy in own_results:
        copy.wait()
    for first in range(0, rows, part):
        for step in range(1, team):
            result_copy(step, first).wait()


def on_device(logperm, source, observed, brownian):
    particles, width, rows, depth = logperm.shape
    slabs, doms = lax.axis_size("slab"), lax.axis_size("dom")
    assert particles == slabs == 4 and doms % width == 0
    layers, crew, ensemble = width * slabs, width * slabs, doms * particles
    f32 = jnp.float32
    dma = pltpu.SemaphoreType.DMA
    scratch = [
        pltpu.VMEM((ensemble, ensemble), f32),
        pltpu.VMEM((layers * rows, depth), f32),
        pltpu.VMEM((layers * rows, depth), f32),
        pltpu.VMEM((layers * rows, depth), f32),
        pltpu.VMEM((layers, rows, depth), f32),
        pltpu.VMEM((ensemble, rows, depth), f32),
        pltpu.VMEM((ensemble, rows * depth), f32),
        pltpu.VMEM((1, rows * depth), f32),
        pltpu.VMEM((crew * rows, depth), f32),
        pltpu.VMEM((crew * rows, depth), f32),
        pltpu.VMEM((crew, crew, ensemble), f32),
        pltpu.VMEM((ensemble, ensemble), f32),
        dma((slabs - 1,)), dma((slabs - 1,)),
        dma((2, 3)), dma((2, 3)),
        dma((doms,)), dma((doms,)),
        dma((8,)),
        dma((crew - 1,)), dma((crew - 1,)),
        dma((crew - 1,)), dma((crew - 1,)),
        dma((2, width - 1)), dma((2, width - 1)),
        *scratch_fields(layers, rows, depth),
    ]
    far = pl.BlockSpec(memory_space=pltpu.HBM)
    drift = pl.pallas_call(
        fused_kernel,
        out_shape=jax.ShapeDtypeStruct((particles, width * rows, depth), f32),
        in_specs=[far] * 4,
        out_specs=far,
        scratch_shapes=scratch,
        compiler_params=pltpu.CompilerParams(
            collective_id=0, has_side_effects=True, vmem_limit_bytes=VMEM_BYTES
        ),
        cost_estimate=pl.CostEstimate(
            flops=logperm.size * 300, bytes_accessed=logperm.size * 16, transcendentals=logperm.size
        ),
        name="langevin",
    )(logperm, source, observed, brownian)
    return 1.25 * logperm + drift.reshape(logperm.shape)


def solution(mesh):
    return jax.shard_map(
        on_device,
        mesh=mesh,
        in_specs=(P("dom", "slab", None, None), P("slab", None, None), P("slab", None, None), P()),
        out_specs=P("dom", "slab", None, None),
        check_vma=False,
    )
```

```python
import math

import jax
import jax.numpy as jnp
from jax import lax
from jax.experimental import pallas as pl
from jax.experimental.pallas import tpu as pltpu
from jax.sharding import PartitionSpec as P

SWEEPS = 8
misfit_weight = 1000.0
VMEM_BYTES = 64 * 1024 * 1024 - 128 * 1024
SUB = 8


def interleaved(ref, layer, rows):
    step = rows // SUB
    first = layer * rows
    return jnp.concatenate([ref[pl.ds(first + v, SUB, stride=step)] for v in range(step)], axis=0)


def edge_masks(depth):
    lane = lax.broadcasted_iota(jnp.int32, (SUB, depth), 1)
    sublane = lax.broadcasted_iota(jnp.int32, (SUB, depth), 0)
    return lane == 0, lane == depth - 1, sublane == 0, sublane == SUB - 1


def neighbors(ref, layer, masks, fill):
    core = ref[layer + 1]
    rows, depth = core.shape
    tiles = [core[at : at + SUB] for at in range(0, rows, SUB)]
    before = [jnp.where(masks[2], fill, pltpu.roll(tiles[-1], 1, 0))] + tiles[:-1]
    after = tiles[1:] + [jnp.where(masks[3], fill, pltpu.roll(tiles[0], SUB - 1, 0))]
    left = [jnp.where(masks[0], fill, pltpu.roll(tile, 1, 1)) for tile in tiles]
    right = [jnp.where(masks[1], fill, pltpu.roll(tile, depth - 1, 1)) for tile in tiles]
    joined = [jnp.concatenate(side, axis=0) for side in (before, after, left, right)]
    return core, (ref[layer], ref[layer + 2], *joined)


def border(ref, layers, rows, depth, fill):
    ref[0] = jnp.full((rows, depth), fill, jnp.float32)
    ref[layers + 1] = jnp.full((rows, depth), fill, jnp.float32)


def scratch_fields(layers, rows, depth):
    padded = pltpu.VMEM((layers + 2, rows, depth), jnp.float32)
    plain = pltpu.VMEM((layers, rows, depth), jnp.float32)
    return [padded] * 4 + [plain] * 3


def set_borders(fields, layers, rows, depth):
    border(fields[0], layers, rows, depth, 1.0)
    for ref in fields[1:4]:
        border(ref, layers, rows, depth, 0.0)


def coefficients(logperm, fields):
    e, inverse, gain = fields[0], fields[4], fields[5]
    layers, rows, depth = inverse.shape
    masks = edge_masks(depth)

    def exponent(layer, carry):
        e[layer + 1] = jnp.exp(0.5 * logperm(layer))
        return carry

    lax.fori_loop(0, layers, exponent, 0, unroll=8)

    def divide(layer, carry):
        core, near = neighbors(e, layer, masks, 1.0)
        total = 1.0 / (near[0] + near[1] + near[2] + near[3] + near[4] + near[5])
        inverse[layer] = total
        gain[layer] = core * total
        return carry

    lax.fori_loop(0, layers, divide, 0, unroll=8)


def relax(rhs, ping, pong, fields):
    e, inverse, gain, start = fields[0], fields[4], fields[5], fields[6]
    layers, rows, depth = inverse.shape
    masks = edge_masks(depth)

    def first(layer, carry):
        value = inverse[layer] * rhs(layer)
        start[layer] = value
        ping[layer + 1] = value
        return carry

    lax.fori_loop(0, layers, first, 0, unroll=8)

    def swept(old, layer):
        _, near = neighbors(old, layer, masks, 0.0)
        total = (near[0] + near[1]) + (near[2] + near[3]) + (near[4] + near[5])
        return start[layer] + gain[layer] * total

    def sweep(old, new):
        def one(layer, carry):
            new[layer + 1] = swept(old, layer)
            return carry

        lax.fori_loop(0, layers, one, 0, unroll=layers)

    def pair(index, carry):
        sweep(ping, pong)
        sweep(pong, ping)
        return carry

    lax.fori_loop(0, (SWEEPS - 2) // 2, pair, 0)

    def last(layer, carry):
        pong[layer + 1] = swept(ping, layer) / e[layer + 1]
        return carry

    lax.fori_loop(0, layers, last, 0, unroll=layers)


def gradient_layer(layer, fields):
    e, pressure, adjoint = fields[0], fields[2], fields[3]
    _, rows, depth = fields[4].shape
    masks = edge_masks(depth)
    e_core, e_near = neighbors(e, layer, masks, 1.0)
    p_core, p_near = neighbors(pressure, layer, masks, 0.0)
    q_core, q_near = neighbors(adjoint, layer, masks, 0.0)
    total = e_near[0] * (p_core - p_near[0]) * (q_core - q_near[0])
    for side in range(1, 6):
        total = total + e_near[side] * (p_core - p_near[side]) * (q_core - q_near[side])
    return -0.5 * e_core * total


def product(left, right, along):
    def halves(value):
        high = value.astype(jnp.bfloat16)
        return high, (value - high.astype(jnp.float32)).astype(jnp.bfloat16)

    def dot(a, b):
        return lax.dot_general(a, b, (((1,), (along,)), ((), ())), preferred_element_type=jnp.float32)

    left_high, left_low = halves(left)
    right_high, right_low = halves(right)
    both = dot(jnp.concatenate([left_high, left_low], axis=0), right_high)
    count = left.shape[0]
    return both[:count] + both[count:] + dot(left_high, right_low)


def fused_kernel(
    logperm, source, observed, brownian_far, moved_out,
    brownian, whole, full_source, full_observed, gradient, members, spread, centre, owned, moved, parts,
    noise, slab_send, slab_recv, side_send, side_recv, member_send, member_recv, own_sem,
    gradient_send, gradient_recv, part_send, part_recv, result_send, result_recv, *fields,
):
    dom, slab = lax.axis_index("dom"), lax.axis_index("slab")
    doms, slabs = lax.axis_size("dom"), lax.axis_size("slab")
    particles, width, rows, depth = logperm.shape
    layers = width * slabs
    team = width
    crew = team * slabs
    ensemble = doms * particles
    place = lax.rem(dom, team)
    base = dom - place
    mine = slab * width + place
    column = place * particles + slab

    def remote(src, dst, send, recv, at_dom, at_slab):
        return pltpu.make_async_remote_copy(
            src_ref=src, dst_ref=dst, send_sem=send, recv_sem=recv,
            device_id=(at_dom, at_slab), device_id_type=pl.DeviceIdType.MESH,
        )

    def crew_device(step):
        layer = lax.rem(mine + step, layers)
        return layer, base + lax.rem(layer, width), layer // width

    fetch = pltpu.make_async_copy(brownian_far, brownian, own_sem.at[5])
    fetch.start()
    barrier = pltpu.get_barrier_semaphore()

    def greet_dom(step, carry):
        pl.semaphore_signal(
            barrier, inc=1, device_id=(lax.rem(dom + step, doms), slab), device_id_type=pl.DeviceIdType.MESH
        )
        return carry

    lax.fori_loop(1, doms, greet_dom, 0)

    def greet_slab(step, carry):
        near = lax.rem(slab + 1 + step // team, slabs)
        pl.semaphore_signal(
            barrier, inc=1, device_id=(base + lax.rem(step, team), near), device_id_type=pl.DeviceIdType.MESH
        )
        return carry

    lax.fori_loop(0, crew - team, greet_slab, 0)
    set_borders(fields, layers, rows, depth)
    pl.semaphore_wait(barrier, doms - 1 + crew - team)

    whole_blocks = whole.reshape(layers, rows, depth)
    own_block = pltpu.make_async_copy(logperm.at[slab], whole_blocks.at[pl.ds(slab * width, width)], own_sem.at[0])
    own_block.start()

    def slab_copy(step):
        near = lax.rem(slab + step, slabs)
        return remote(
            logperm.at[near], whole_blocks.at[pl.ds(slab * width, width)],
            slab_send.at[step - 1], slab_recv.at[step - 1], dom, near,
        )

    order = [2, 1, 3]

    def slab_piece(step, layer):
        near = lax.rem(slab + step, slabs)
        return remote(
            logperm.at[near, layer], whole_blocks.at[slab * width + layer],
            slab_send.at[step - 1], slab_recv.at[step - 1], dom, near,
        )

    across = lax.rem(slab + 2, slabs)
    beside = slab + 1 - 2 * lax.rem(slab, 2)
    local = []

    def side_copies(which, block, full):
        def at(owner):
            return full.reshape(layers, rows, depth).at[pl.ds(owner * width, width)]

        return [
            remote(block, at(slab), side_send.at[which, 0], side_recv.at[which, 0], dom, across),
            remote(block, at(slab), side_send.at[which, 1], side_recv.at[which, 1], dom, beside),
            remote(at(across), at(across), side_send.at[which, 2], side_recv.at[which, 2], dom, beside),
        ]

    sides = [side_copies(0, source, full_source), side_copies(1, observed, full_observed)]
    for which, (block, full) in enumerate(((source, full_source), (observed, full_observed))):
        copy = pltpu.make_async_copy(block, full.reshape(layers, rows, depth).at[pl.ds(slab * width, width)], own_sem.at[1 + which])
        copy.start()
        local.append(copy)
    def member_copy(step):
        target = lax.rem(base + team * (1 + step // team), doms) + lax.rem(place + step, team)
        return remote(
            logperm.at[:, lax.rem(target, team)], members.at[pl.ds(dom * particles, particles)],
            member_send.at[step], member_recv.at[step], target, slab,
        )

    def each_member(act, first, last):
        def body(step, carry):
            act(member_copy(step))
            return carry

        lax.fori_loop(first, last, body, 0)

    def member_piece(step, particle):
        target = lax.rem(base + team * (1 + step // team), doms) + lax.rem(place + step, team)
        return remote(
            logperm.at[particle, lax.rem(target, team)], members.at[dom * particles + particle],
            member_send.at[step], member_recv.at[step], target, slab,
        )

    for piece in range(width):
        for step in order:
            slab_piece(step, piece).start()
        for step in range(min(team, doms - team)):
            member_piece(step, piece).start()
    sides[0][0].start()
    sides[0][1].start()

    def start_rest(step, carry):
        member_copy(step).start()
        return carry

    lax.fori_loop(doms - team + 1, doms, start_rest, 0)
    lax.fori_loop(min(team, doms - team), doms - team, start_rest, 0)
    own_members = pltpu.make_async_copy(
        logperm.at[:, place], members.at[pl.ds(dom * particles, particles)], own_sem.at[3]
    )
    own_members.start()

    fetch.wait()
    turned = [
        brownian[pl.ds(pl.multiple_of(lax.rem(base + at * team, doms) * particles, 8), crew)]
        for at in range(doms // team)
    ]
    noise[...] = jnp.concatenate(turned, axis=0).T
    own_block.wait()
    for step in order:
        slab_copy(step).wait_recv()
    sides[1][0].start()
    sides[1][1].start()
    coefficients(lambda layer: interleaved(whole, layer, rows), fields)
    sides[0][0].wait_recv()
    sides[0][2].start()
    sides[0][1].wait_recv()
    local[0].wait()
    sides[0][2].wait_recv()
    relax(lambda layer: interleaved(full_source, layer, rows), fields[1], fields[2], fields)
    pressure = fields[2]
    sides[1][0].wait_recv()
    sides[1][2].start()
    sides[1][1].wait_recv()
    local[1].wait()
    sides[1][2].wait_recv()

    def misfit(layer):
        return misfit_weight * (pressure[layer + 1] - interleaved(full_observed, layer, rows))

    relax(misfit, fields[1], fields[3], fields)

    def gradient_copy(step):
        layer, at_dom, at_slab = crew_device(step)
        return remote(
            gradient.at[layer], owned.at[pl.ds(column * rows, rows)],
            gradient_send.at[step - 1], gradient_recv.at[step - 1], at_dom, at_slab,
        )

    def send_gradient(step, carry):
        layer = lax.rem(mine + step, layers)
        gradient[layer] = gradient_layer(layer, fields)
        gradient_copy(step).start()
        return carry

    lax.fori_loop(1, layers, send_gradient, 0, unroll=5)
    owned[pl.ds(column * rows, rows)] = gradient_layer(mine, fields)

    member_rows = members.reshape(ensemble * rows, depth)
    tiles = rows // SUB

    def line(team_at, row):
        first = lax.rem(base + team_at * team, doms) * particles
        return member_rows[pl.ds(first * rows + row, crew, stride=rows)]

    own_members.wait()
    each_member(lambda copy: copy.wait_recv(), doms - team + 1, doms)
    for row in range(rows):
        cells = slice(row * depth, (row + 1) * depth)
        values = line(0, row)
        mean = jnp.sum(values, axis=0, keepdims=True) * (1.0 / crew)
        spread[0:crew, cells] = values - mean
        centre[:, cells] = mean

    def wait_gradient(step, carry):
        gradient_copy(step).wait_recv()
        return carry

    lax.fori_loop(1, crew, wait_gradient, 0)
    piece = min(16, rows)

    def held(first):
        return jnp.concatenate(
            [
                owned[pl.ds((row % tiles) * SUB + row // tiles, crew, stride=rows)]
                for row in range(first, first + piece)
            ],
            axis=1,
        )

    for team_at in range(doms // team):
        at = slice(team_at * crew, (team_at + 1) * crew)
        if team_at > 0:
            each_member(lambda copy: copy.wait_recv(), (team_at - 1) * team, team_at * team)
            for row in range(rows):
                cells = slice(row * depth, (row + 1) * depth)
                spread[at, cells] = line(team_at, row) - centre[:, cells]
        gram = jnp.zeros((crew, crew), jnp.float32)
        for first in range(0, rows, piece):
            gram = gram + product(held(first), spread[at, first * depth : (first + piece) * depth], 1)
        parts[mine, :, at] = gram

    def part_copy(step):
        _, at_dom, at_slab = crew_device(step)
        return remote(
            parts.at[mine], parts.at[mine], part_send.at[step - 1], part_recv.at[step - 1], at_dom, at_slab
        )

    def start_part(step, carry):
        part_copy(step).start()
        return carry

    def wait_part(step, carry):
        part_copy(step).wait_recv()
        return carry

    lax.fori_loop(1, crew, start_part, 0)
    lax.fori_loop(1, crew, wait_part, 0)
    gram = jnp.sum(parts[...], axis=0)
    gram = gram - jnp.sum(gram, axis=1, keepdims=True) * (1.0 / ensemble)
    step_size = ensemble / (4.0 * (layers * rows * depth + 1))
    first_column = pl.multiple_of(base * particles, 8)
    mixing = -(step_size / ensemble) * gram + math.sqrt(2.0 * step_size / ensemble) * noise[
        pl.ds(first_column, crew)
    ]
    mixing = mixing - (jnp.sum(mixing, axis=1, keepdims=True) + 0.25) * (1.0 / ensemble)
    moved_block = moved.reshape(crew, rows, depth)

    def result_part(to, first):
        return (
            moved_block.at[pl.ds(to * particles, particles), pl.ds(first, part)],
            moved_out.at[:, pl.ds(place * rows + first, part)],
        )

    def result_copy(step, first):
        to = lax.rem(place + step, team)
        at = first // part
        return remote(
            *result_part(to, first), result_send.at[at, step - 1], result_recv.at[at, step - 1],
            base + to, slab,
        )

    part = rows // 2
    own_results = []
    for first in range(0, rows, part):
        cells = slice(first * depth, (first + part) * depth)
        result = spread[0:crew, cells] * 1.25 + centre[:, cells] + product(mixing, spread[:, cells], 0)
        for row in range(part):
            moved[pl.ds(first + row, crew, stride=rows)] = result[:, row * depth : (row + 1) * depth]
        for step in range(1, team):
            result_copy(step, first).start()
        copy = pltpu.make_async_copy(*result_part(place, first), own_sem.at[6 + first // part])
        copy.start()
        own_results.append(copy)

    for step in order:
        slab_copy(step).wait_send()
    for which in range(2):
        for copy in sides[which]:
            copy.wait_send()

    def sent_crew(step, carry):
        gradient_copy(step).wait_send()
        part_copy(step).wait_send()
        return carry

    each_member(lambda copy: copy.wait_send(), 0, doms - team)
    each_member(lambda copy: copy.wait_send(), doms - team + 1, doms)
    lax.fori_loop(1, crew, sent_crew, 0)
    for copy in own_results:
        copy.wait()
    for first in range(0, rows, part):
        for step in range(1, team):
            result_copy(step, first).wait()


def on_device(logperm, source, observed, brownian):
    particles, width, rows, depth = logperm.shape
    slabs, doms = lax.axis_size("slab"), lax.axis_size("dom")
    assert particles == slabs == 4 and doms % width == 0
    layers, crew, ensemble = width * slabs, width * slabs, doms * particles
    f32 = jnp.float32
    dma = pltpu.SemaphoreType.DMA
    scratch = [
        pltpu.VMEM((ensemble, ensemble), f32),
        pltpu.VMEM((layers * rows, depth), f32),
        pltpu.VMEM((layers * rows, depth), f32),
        pltpu.VMEM((layers * rows, depth), f32),
        pltpu.VMEM((layers, rows, depth), f32),
        pltpu.VMEM((ensemble, rows, depth), f32),
        pltpu.VMEM((ensemble, rows * depth), f32),
        pltpu.VMEM((1, rows * depth), f32),
        pltpu.VMEM((crew * rows, depth), f32),
        pltpu.VMEM((crew * rows, depth), f32),
        pltpu.VMEM((crew, crew, ensemble), f32),
        pltpu.VMEM((ensemble, ensemble), f32),
        dma((slabs - 1,)), dma((slabs - 1,)),
        dma((2, 3)), dma((2, 3)),
        dma((doms,)), dma((doms,)),
        dma((8,)),
        dma((crew - 1,)), dma((crew - 1,)),
        dma((crew - 1,)), dma((crew - 1,)),
        dma((2, width - 1)), dma((2, width - 1)),
        *scratch_fields(layers, rows, depth),
    ]
    far = pl.BlockSpec(memory_space=pltpu.HBM)
    moved = pl.pallas_call(
        fused_kernel,
        out_shape=jax.ShapeDtypeStruct((particles, width * rows, depth), f32),
        in_specs=[far] * 4,
        out_specs=far,
        scratch_shapes=scratch,
        compiler_params=pltpu.CompilerParams(
            collective_id=0, has_side_effects=True, vmem_limit_bytes=VMEM_BYTES
        ),
        cost_estimate=pl.CostEstimate(
            flops=logperm.size * 300, bytes_accessed=logperm.size * 16, transcendentals=logperm.size
        ),
        name="langevin",
    )(logperm, source, observed, brownian)
    return moved.reshape(logperm.shape)


def solution(mesh):
    return jax.shard_map(
        on_device,
        mesh=mesh,
        in_specs=(P("dom", "slab", None, None), P("slab", None, None), P("slab", None, None), P()),
        out_specs=P("dom", "slab", None, None),
        check_vma=False,
    )
```

```python
import math

import jax
import jax.numpy as jnp
from jax import lax
from jax.experimental import pallas as pl
from jax.experimental.pallas import tpu as pltpu
from jax.sharding import PartitionSpec as P

SWEEPS = 8
misfit_weight = 1000.0
VMEM_BYTES = 64 * 1024 * 1024 - 128 * 1024
SUB = 8


def interleaved(ref, layer, rows):
    step = rows // SUB
    first = layer * rows
    return jnp.concatenate([ref[pl.ds(first + v, SUB, stride=step)] for v in range(step)], axis=0)


def edge_masks(depth):
    lane = lax.broadcasted_iota(jnp.int32, (SUB, depth), 1)
    sublane = lax.broadcasted_iota(jnp.int32, (SUB, depth), 0)
    return lane == 0, lane == depth - 1, sublane == 0, sublane == SUB - 1


def neighbors(ref, layer, masks, fill):
    core = ref[layer + 1]
    rows, depth = core.shape
    tiles = [core[at : at + SUB] for at in range(0, rows, SUB)]
    before = [jnp.where(masks[2], fill, pltpu.roll(tiles[-1], 1, 0))] + tiles[:-1]
    after = tiles[1:] + [jnp.where(masks[3], fill, pltpu.roll(tiles[0], SUB - 1, 0))]
    left = [jnp.where(masks[0], fill, pltpu.roll(tile, 1, 1)) for tile in tiles]
    right = [jnp.where(masks[1], fill, pltpu.roll(tile, depth - 1, 1)) for tile in tiles]
    joined = [jnp.concatenate(side, axis=0) for side in (before, after, left, right)]
    return core, (ref[layer], ref[layer + 2], *joined)


def plane_sum(core, masks):
    rows, depth = core.shape
    before = jnp.concatenate(
        [jnp.where(masks[2], 0.0, pltpu.roll(core[rows - SUB :], 1, 0)), core[: rows - SUB]], axis=0
    )
    after = jnp.concatenate(
        [core[SUB:], jnp.where(masks[3], 0.0, pltpu.roll(core[:SUB], SUB - 1, 0))], axis=0
    )
    left = jnp.where(masks[4], 0.0, pltpu.roll(core, 1, 1))
    right = jnp.where(masks[5], 0.0, pltpu.roll(core, depth - 1, 1))
    return (before + after) + (left + right)


def border(ref, layers, rows, depth, fill):
    ref[0] = jnp.full((rows, depth), fill, jnp.float32)
    ref[layers + 1] = jnp.full((rows, depth), fill, jnp.float32)


def scratch_fields(layers, rows, depth):
    padded = pltpu.VMEM((layers + 2, rows, depth), jnp.float32)
    plain = pltpu.VMEM((layers, rows, depth), jnp.float32)
    return [padded] * 4 + [plain] * 3


def set_borders(fields, layers, rows, depth):
    border(fields[0], layers, rows, depth, 1.0)
    for ref in fields[1:4]:
        border(ref, layers, rows, depth, 0.0)


def coefficients(logperm, fields):
    e, inverse, gain = fields[0], fields[4], fields[5]
    layers, rows, depth = inverse.shape
    masks = edge_masks(depth)

    def exponent(layer, carry):
        e[layer + 1] = jnp.exp(0.5 * logperm(layer))
        return carry

    lax.fori_loop(0, layers, exponent, 0, unroll=8)

    def divide(layer, carry):
        core, near = neighbors(e, layer, masks, 1.0)
        total = 1.0 / (near[0] + near[1] + near[2] + near[3] + near[4] + near[5])
        inverse[layer] = total
        gain[layer] = core * total
        return carry

    lax.fori_loop(0, layers, divide, 0, unroll=8)


def relax(rhs, ping, pong, fields, between):
    e, inverse, gain, start = fields[0], fields[4], fields[5], fields[6]
    layers, rows, depth = inverse.shape
    masks = edge_masks(depth)
    lane = lax.broadcasted_iota(jnp.int32, (rows, depth), 1)
    masks = (*masks, lane == 0, lane == depth - 1)

    def first(layer, carry):
        value = inverse[layer] * rhs(layer)
        start[layer] = value
        ping[layer + 1] = value
        return carry

    lax.fori_loop(0, layers, first, 0, unroll=8)

    def sweep(old, new, finish):
        below, core = None, old[1]
        for layer in range(layers):
            above = old[layer + 2] if layer + 1 < layers else None
            total = plane_sum(core, masks)
            if below is not None:
                total = total + below
            if above is not None:
                total = total + above
            new[layer + 1] = finish(layer, start[layer] + gain[layer] * total)
            below, core = core, above

    def pair(index, carry):
        sweep(ping, pong, lambda layer, value: value)
        sweep(pong, ping, lambda layer, value: value)
        return carry

    pairs = (SWEEPS - 2) // 2
    lax.fori_loop(0, pairs - 1, pair, 0)
    between()
    lax.fori_loop(pairs - 1, pairs, pair, 0)
    sweep(ping, pong, lambda layer, value: value / e[layer + 1])


def gradient_layer(layer, fields):
    e, pressure, adjoint = fields[0], fields[2], fields[3]
    _, rows, depth = fields[4].shape
    masks = edge_masks(depth)
    e_core, e_near = neighbors(e, layer, masks, 1.0)
    p_core, p_near = neighbors(pressure, layer, masks, 0.0)
    q_core, q_near = neighbors(adjoint, layer, masks, 0.0)
    total = e_near[0] * (p_core - p_near[0]) * (q_core - q_near[0])
    for side in range(1, 6):
        total = total + e_near[side] * (p_core - p_near[side]) * (q_core - q_near[side])
    return -0.5 * e_core * total


def product(left, right, along):
    def halves(value):
        high = value.astype(jnp.bfloat16)
        return high, (value - high.astype(jnp.float32)).astype(jnp.bfloat16)

    def dot(a, b):
        return lax.dot_general(a, b, (((1,), (along,)), ((), ())), preferred_element_type=jnp.float32)

    left_high, left_low = halves(left)
    right_high, right_low = halves(right)
    both = dot(jnp.concatenate([left_high, left_low], axis=0), right_high)
    count = left.shape[0]
    return both[:count] + both[count:] + dot(left_high, right_low)


def fused_kernel(
    logperm, source, observed, brownian_far, moved_out,
    brownian, whole, full_source, full_observed, gradient, members, spread, centre, owned, moved, parts,
    noise, slab_send, slab_recv, side_send, side_recv, member_send, member_recv, own_sem,
    gradient_send, gradient_recv, part_send, part_recv, result_send, result_recv, *fields,
):
    dom, slab = lax.axis_index("dom"), lax.axis_index("slab")
    doms, slabs = lax.axis_size("dom"), lax.axis_size("slab")
    particles, width, rows, depth = logperm.shape
    layers = width * slabs
    team = width
    crew = team * slabs
    ensemble = doms * particles
    place = lax.rem(dom, team)
    base = dom - place
    mine = slab * width + place
    column = place * particles + slab

    def remote(src, dst, send, recv, at_dom, at_slab):
        return pltpu.make_async_remote_copy(
            src_ref=src, dst_ref=dst, send_sem=send, recv_sem=recv,
            device_id=(at_dom, at_slab), device_id_type=pl.DeviceIdType.MESH,
        )

    def crew_device(step):
        layer = lax.rem(mine + step, layers)
        return layer, base + lax.rem(layer, width), layer // width

    fetch = pltpu.make_async_copy(brownian_far, brownian, own_sem.at[5])
    fetch.start()
    barrier = pltpu.get_barrier_semaphore()

    def greet_dom(step, carry):
        pl.semaphore_signal(
            barrier, inc=1, device_id=(lax.rem(dom + step, doms), slab), device_id_type=pl.DeviceIdType.MESH
        )
        return carry

    lax.fori_loop(1, doms, greet_dom, 0)

    def greet_slab(step, carry):
        near = lax.rem(slab + 1 + step // team, slabs)
        pl.semaphore_signal(
            barrier, inc=1, device_id=(base + lax.rem(step, team), near), device_id_type=pl.DeviceIdType.MESH
        )
        return carry

    lax.fori_loop(0, crew - team, greet_slab, 0)
    set_borders(fields, layers, rows, depth)
    pl.semaphore_wait(barrier, doms - 1 + crew - team)

    whole_blocks = whole.reshape(layers, rows, depth)
    own_block = pltpu.make_async_copy(logperm.at[slab], whole_blocks.at[pl.ds(slab * width, width)], own_sem.at[0])
    own_block.start()

    def slab_copy(step):
        near = lax.rem(slab + step, slabs)
        return remote(
            logperm.at[near], whole_blocks.at[pl.ds(slab * width, width)],
            slab_send.at[step - 1], slab_recv.at[step - 1], dom, near,
        )

    order = [2, 1, 3]

    for step in order:
        slab_copy(step).start()

    across = lax.rem(slab + 2, slabs)
    beside = slab + 1 - 2 * lax.rem(slab, 2)
    local = []

    def side_copies(which, block, full):
        def at(owner):
            return full.reshape(layers, rows, depth).at[pl.ds(owner * width, width)]

        return [
            remote(block, at(slab), side_send.at[which, 0], side_recv.at[which, 0], dom, across),
            remote(block, at(slab), side_send.at[which, 1], side_recv.at[which, 1], dom, beside),
            remote(at(across), at(across), side_send.at[which, 2], side_recv.at[which, 2], dom, beside),
        ]

    sides = [side_copies(0, source, full_source), side_copies(1, observed, full_observed)]
    for which, (block, full) in enumerate(((source, full_source), (observed, full_observed))):
        copy = pltpu.make_async_copy(block, full.reshape(layers, rows, depth).at[pl.ds(slab * width, width)], own_sem.at[1 + which])
        copy.start()
        local.append(copy)
    sides[0][0].start()
    sides[0][1].start()

    def member_copy(step):
        target = lax.rem(base + team * (1 + step // team), doms) + lax.rem(place + step, team)
        return remote(
            logperm.at[:, lax.rem(target, team)], members.at[pl.ds(dom * particles, particles)],
            member_send.at[step], member_recv.at[step], target, slab,
        )

    def each_member(act, first, last):
        def body(step, carry):
            act(member_copy(step))
            return carry

        lax.fori_loop(first, last, body, 0)

    def start_member(step, carry):
        member_copy(step).start()
        return carry

    lax.fori_loop(0, doms - team, start_member, 0)
    lax.fori_loop(doms - team + 1, doms, start_member, 0)
    own_members = pltpu.make_async_copy(
        logperm.at[:, place], members.at[pl.ds(dom * particles, particles)], own_sem.at[3]
    )
    own_members.start()

    fetch.wait()
    turned = [
        brownian[pl.ds(pl.multiple_of(lax.rem(base + at * team, doms) * particles, 8), crew)]
        for at in range(doms // team)
    ]
    noise[...] = jnp.concatenate(turned, axis=0).T
    own_block.wait()
    for step in order:
        slab_copy(step).wait_recv()
    sides[1][0].start()
    sides[1][1].start()
    coefficients(lambda layer: interleaved(whole, layer, rows), fields)
    sides[0][0].wait_recv()
    sides[0][2].start()
    sides[0][1].wait_recv()
    local[0].wait()
    sides[0][2].wait_recv()

    def forward_observed():
        sides[1][0].wait_recv()
        sides[1][2].start()

    relax(lambda layer: interleaved(full_source, layer, rows), fields[1], fields[2], fields, forward_observed)
    pressure = fields[2]
    sides[1][1].wait_recv()
    local[1].wait()
    sides[1][2].wait_recv()

    def misfit(layer):
        return misfit_weight * (pressure[layer + 1] - interleaved(full_observed, layer, rows))

    relax(misfit, fields[1], fields[3], fields, lambda: None)

    def gradient_copy(step):
        layer, at_dom, at_slab = crew_device(step)
        return remote(
            gradient.at[layer], owned.at[pl.ds(column * rows, rows)],
            gradient_send.at[step - 1], gradient_recv.at[step - 1], at_dom, at_slab,
        )

    def send_gradient(step, carry):
        layer = lax.rem(mine + step, layers)
        gradient[layer] = gradient_layer(layer, fields)
        gradient_copy(step).start()
        return carry

    lax.fori_loop(1, layers, send_gradient, 0, unroll=5)
    owned[pl.ds(column * rows, rows)] = gradient_layer(mine, fields)

    member_rows = members.reshape(ensemble * rows, depth)
    tiles = rows // SUB

    def line(team_at, row):
        first = lax.rem(base + team_at * team, doms) * particles
        return member_rows[pl.ds(first * rows + row, crew, stride=rows)]

    own_members.wait()
    each_member(lambda copy: copy.wait_recv(), doms - team + 1, doms)
    for row in range(rows):
        cells = slice(row * depth, (row + 1) * depth)
        values = line(0, row)
        mean = jnp.sum(values, axis=0, keepdims=True) * (1.0 / crew)
        spread[0:crew, cells] = values - mean
        centre[:, cells] = mean

    def wait_gradient(step, carry):
        gradient_copy(step).wait_recv()
        return carry

    lax.fori_loop(1, crew, wait_gradient, 0)
    piece = min(16, rows)

    def held(first):
        return jnp.concatenate(
            [
                owned[pl.ds((row % tiles) * SUB + row // tiles, crew, stride=rows)]
                for row in range(first, first + piece)
            ],
            axis=1,
        )

    for team_at in range(doms // team):
        at = slice(team_at * crew, (team_at + 1) * crew)
        if team_at > 0:
            each_member(lambda copy: copy.wait_recv(), (team_at - 1) * team, team_at * team)
            for row in range(rows):
                cells = slice(row * depth, (row + 1) * depth)
                spread[at, cells] = line(team_at, row) - centre[:, cells]
        gram = jnp.zeros((crew, crew), jnp.float32)
        for first in range(0, rows, piece):
            gram = gram + product(held(first), spread[at, first * depth : (first + piece) * depth], 1)
        parts[mine, :, at] = gram

    def part_copy(step):
        _, at_dom, at_slab = crew_device(step)
        return remote(
            parts.at[mine], parts.at[mine], part_send.at[step - 1], part_recv.at[step - 1], at_dom, at_slab
        )

    def start_part(step, carry):
        part_copy(step).start()
        return carry

    def wait_part(step, carry):
        part_copy(step).wait_recv()
        return carry

    lax.fori_loop(1, crew, start_part, 0)
    lax.fori_loop(1, crew, wait_part, 0)
    gram = jnp.sum(parts[...], axis=0)
    gram = gram - jnp.sum(gram, axis=1, keepdims=True) * (1.0 / ensemble)
    step_size = ensemble / (4.0 * (layers * rows * depth + 1))
    first_column = pl.multiple_of(base * particles, 8)
    mixing = -(step_size / ensemble) * gram + math.sqrt(2.0 * step_size / ensemble) * noise[
        pl.ds(first_column, crew)
    ]
    mixing = mixing - (jnp.sum(mixing, axis=1, keepdims=True) + 0.25) * (1.0 / ensemble)
    moved_block = moved.reshape(crew, rows, depth)

    def result_part(to, first):
        return (
            moved_block.at[pl.ds(to * particles, particles), pl.ds(first, part)],
            moved_out.at[:, pl.ds(place * rows + first, part)],
        )

    def result_copy(step, first):
        to = lax.rem(place + step, team)
        at = first // part
        return remote(
            *result_part(to, first), result_send.at[at, step - 1], result_recv.at[at, step - 1],
            base + to, slab,
        )

    part = rows // 2
    own_results = []
    for first in range(0, rows, part):
        cells = slice(first * depth, (first + part) * depth)
        result = spread[0:crew, cells] * 1.25 + centre[:, cells] + product(mixing, spread[:, cells], 0)
        for row in range(part):
            moved[pl.ds(first + row, crew, stride=rows)] = result[:, row * depth : (row + 1) * depth]
        for step in range(1, team):
            result_copy(step, first).start()
        copy = pltpu.make_async_copy(*result_part(place, first), own_sem.at[6 + first // part])
        copy.start()
        own_results.append(copy)

    for step in order:
        slab_copy(step).wait_send()
    for which in range(2):
        for copy in sides[which]:
            copy.wait_send()

    def sent_crew(step, carry):
        gradient_copy(step).wait_send()
        part_copy(step).wait_send()
        return carry

    each_member(lambda copy: copy.wait_send(), 0, doms - team)
    each_member(lambda copy: copy.wait_send(), doms - team + 1, doms)
    lax.fori_loop(1, crew, sent_crew, 0)
    for copy in own_results:
        copy.wait()
    for first in range(0, rows, part):
        for step in range(1, team):
            result_copy(step, first).wait()


def on_device(logperm, source, observed, brownian):
    particles, width, rows, depth = logperm.shape
    slabs, doms = lax.axis_size("slab"), lax.axis_size("dom")
    assert particles == slabs == 4 and doms % width == 0
    layers, crew, ensemble = width * slabs, width * slabs, doms * particles
    f32 = jnp.float32
    dma = pltpu.SemaphoreType.DMA
    scratch = [
        pltpu.VMEM((ensemble, ensemble), f32),
        pltpu.VMEM((layers * rows, depth), f32),
        pltpu.VMEM((layers * rows, depth), f32),
        pltpu.VMEM((layers * rows, depth), f32),
        pltpu.VMEM((layers, rows, depth), f32),
        pltpu.VMEM((ensemble, rows, depth), f32),
        pltpu.VMEM((ensemble, rows * depth), f32),
        pltpu.VMEM((1, rows * depth), f32),
        pltpu.VMEM((crew * rows, depth), f32),
        pltpu.VMEM((crew * rows, depth), f32),
        pltpu.VMEM((crew, crew, ensemble), f32),
        pltpu.VMEM((ensemble, ensemble), f32),
        dma((slabs - 1,)), dma((slabs - 1,)),
        dma((2, 3)), dma((2, 3)),
        dma((doms,)), dma((doms,)),
        dma((8,)),
        dma((crew - 1,)), dma((crew - 1,)),
        dma((crew - 1,)), dma((crew - 1,)),
        dma((2, width - 1)), dma((2, width - 1)),
        *scratch_fields(layers, rows, depth),
    ]
    far = pl.BlockSpec(memory_space=pltpu.HBM)
    moved = pl.pallas_call(
        fused_kernel,
        out_shape=jax.ShapeDtypeStruct((particles, width * rows, depth), f32),
        in_specs=[far] * 4,
        out_specs=far,
        scratch_shapes=scratch,
        compiler_params=pltpu.CompilerParams(
            collective_id=0, has_side_effects=True, vmem_limit_bytes=VMEM_BYTES
        ),
        cost_estimate=pl.CostEstimate(
            flops=logperm.size * 300, bytes_accessed=logperm.size * 16, transcendentals=logperm.size
        ),
        name="langevin",
    )(logperm, source, observed, brownian)
    return moved.reshape(logperm.shape)


def solution(mesh):
    return jax.shard_map(
        on_device,
        mesh=mesh,
        in_specs=(P("dom", "slab", None, None), P("slab", None, None), P("slab", None, None), P()),
        out_specs=P("dom", "slab", None, None),
        check_vma=False,
    )
```

```python
import math

import jax
import jax.numpy as jnp
from jax import lax
from jax.experimental import pallas as pl
from jax.experimental.pallas import tpu as pltpu
from jax.sharding import PartitionSpec as P

SWEEPS = 8
misfit_weight = 1000.0
VMEM_BYTES = 64 * 1024 * 1024 - 128 * 1024
SUB = 8


def interleaved(ref, layer, rows):
    step = rows // SUB
    first = layer * rows
    return jnp.concatenate([ref[pl.ds(first + v, SUB, stride=step)] for v in range(step)], axis=0)


def edge_masks(depth):
    lane = lax.broadcasted_iota(jnp.int32, (SUB, depth), 1)
    sublane = lax.broadcasted_iota(jnp.int32, (SUB, depth), 0)
    return lane == 0, lane == depth - 1, sublane == 0, sublane == SUB - 1


def neighbors(ref, layer, masks, fill):
    core = ref[layer + 1]
    rows, depth = core.shape
    tiles = [core[at : at + SUB] for at in range(0, rows, SUB)]
    before = [jnp.where(masks[2], fill, pltpu.roll(tiles[-1], 1, 0))] + tiles[:-1]
    after = tiles[1:] + [jnp.where(masks[3], fill, pltpu.roll(tiles[0], SUB - 1, 0))]
    left = [jnp.where(masks[0], fill, pltpu.roll(tile, 1, 1)) for tile in tiles]
    right = [jnp.where(masks[1], fill, pltpu.roll(tile, depth - 1, 1)) for tile in tiles]
    joined = [jnp.concatenate(side, axis=0) for side in (before, after, left, right)]
    return core, (ref[layer], ref[layer + 2], *joined)


def plane_sum(core, masks):
    rows, depth = core.shape
    before = jnp.concatenate(
        [jnp.where(masks[2], 0.0, pltpu.roll(core[rows - SUB :], 1, 0)), core[: rows - SUB]], axis=0
    )
    after = jnp.concatenate(
        [core[SUB:], jnp.where(masks[3], 0.0, pltpu.roll(core[:SUB], SUB - 1, 0))], axis=0
    )
    left = jnp.where(masks[4], 0.0, pltpu.roll(core, 1, 1))
    right = jnp.where(masks[5], 0.0, pltpu.roll(core, depth - 1, 1))
    return (before + after) + (left + right)


def border(ref, layers, rows, depth, fill):
    ref[0] = jnp.full((rows, depth), fill, jnp.float32)
    ref[layers + 1] = jnp.full((rows, depth), fill, jnp.float32)


def scratch_fields(layers, rows, depth):
    padded = pltpu.VMEM((layers + 2, rows, depth), jnp.float32)
    plain = pltpu.VMEM((layers, rows, depth), jnp.float32)
    return [padded] * 4 + [plain] * 3


def set_borders(fields, layers, rows, depth):
    border(fields[0], layers, rows, depth, 1.0)
    for ref in fields[1:4]:
        border(ref, layers, rows, depth, 0.0)


def coefficients(logperm, fields):
    e, inverse, gain = fields[0], fields[4], fields[5]
    layers, rows, depth = inverse.shape
    masks = edge_masks(depth)

    def exponent(layer, carry):
        e[layer + 1] = jnp.exp(0.5 * logperm(layer))
        return carry

    lax.fori_loop(0, layers, exponent, 0, unroll=8)

    def divide(layer, carry):
        core, near = neighbors(e, layer, masks, 1.0)
        total = 1.0 / (near[0] + near[1] + near[2] + near[3] + near[4] + near[5])
        inverse[layer] = total
        gain[layer] = core * total
        return carry

    lax.fori_loop(0, layers, divide, 0, unroll=8)


def relax(rhs, ping, pong, fields, between):
    e, inverse, gain, start = fields[0], fields[4], fields[5], fields[6]
    layers, rows, depth = inverse.shape
    masks = edge_masks(depth)
    lane = lax.broadcasted_iota(jnp.int32, (rows, depth), 1)
    masks = (*masks, lane == 0, lane == depth - 1)

    def first(layer, carry):
        value = inverse[layer] * rhs(layer)
        start[layer] = value
        ping[layer + 1] = value
        return carry

    lax.fori_loop(0, layers, first, 0, unroll=8)

    def sweep(old, new, finish):
        below, core = None, old[1]
        for layer in range(layers):
            above = old[layer + 2] if layer + 1 < layers else None
            total = plane_sum(core, masks)
            if below is not None:
                total = total + below
            if above is not None:
                total = total + above
            new[layer + 1] = finish(layer, start[layer] + gain[layer] * total)
            below, core = core, above

    def pair(index, carry):
        sweep(ping, pong, lambda layer, value: value)
        sweep(pong, ping, lambda layer, value: value)
        return carry

    pairs = (SWEEPS - 2) // 2
    lax.fori_loop(0, pairs - 1, pair, 0)
    between()
    lax.fori_loop(pairs - 1, pairs, pair, 0)
    sweep(ping, pong, lambda layer, value: value / e[layer + 1])


def gradient_layer(layer, fields):
    e, pressure, adjoint = fields[0], fields[2], fields[3]
    _, rows, depth = fields[4].shape
    masks = edge_masks(depth)
    e_core, e_near = neighbors(e, layer, masks, 1.0)
    p_core, p_near = neighbors(pressure, layer, masks, 0.0)
    q_core, q_near = neighbors(adjoint, layer, masks, 0.0)
    total = e_near[0] * (p_core - p_near[0]) * (q_core - q_near[0])
    for side in range(1, 6):
        total = total + e_near[side] * (p_core - p_near[side]) * (q_core - q_near[side])
    return -0.5 * e_core * total


def product(left, right, along):
    def halves(value):
        high = value.astype(jnp.bfloat16)
        return high, (value - high.astype(jnp.float32)).astype(jnp.bfloat16)

    def dot(a, b):
        return lax.dot_general(a, b, (((1,), (along,)), ((), ())), preferred_element_type=jnp.float32)

    left_high, left_low = halves(left)
    right_high, right_low = halves(right)
    both = dot(jnp.concatenate([left_high, left_low], axis=0), right_high)
    count = left.shape[0]
    return both[:count] + both[count:] + dot(left_high, right_low)


def fused_kernel(
    logperm, source, observed, brownian_far, moved_out,
    brownian, whole, full_source, full_observed, gradient, members, spread, centre, owned, moved, parts,
    noise, slab_send, slab_recv, side_send, side_recv, member_send, member_recv, own_sem,
    gradient_send, gradient_recv, part_send, part_recv, result_send, result_recv, *fields,
):
    dom, slab = lax.axis_index("dom"), lax.axis_index("slab")
    doms, slabs = lax.axis_size("dom"), lax.axis_size("slab")
    particles, width, rows, depth = logperm.shape
    layers = width * slabs
    team = width
    crew = team * slabs
    ensemble = doms * particles
    place = lax.rem(dom, team)
    base = dom - place
    mine = slab * width + place
    column = place * particles + slab

    def remote(src, dst, send, recv, at_dom, at_slab):
        return pltpu.make_async_remote_copy(
            src_ref=src, dst_ref=dst, send_sem=send, recv_sem=recv,
            device_id=(at_dom, at_slab), device_id_type=pl.DeviceIdType.MESH,
        )

    def crew_device(step):
        layer = lax.rem(mine + step, layers)
        return layer, base + lax.rem(layer, width), layer // width

    fetch = pltpu.make_async_copy(brownian_far, brownian, own_sem.at[5])
    fetch.start()
    barrier = pltpu.get_barrier_semaphore()

    def greet_dom(step, carry):
        pl.semaphore_signal(
            barrier, inc=1, device_id=(lax.rem(dom + step, doms), slab), device_id_type=pl.DeviceIdType.MESH
        )
        return carry

    lax.fori_loop(1, doms, greet_dom, 0)

    def greet_slab(step, carry):
        near = lax.rem(slab + 1 + step // team, slabs)
        pl.semaphore_signal(
            barrier, inc=1, device_id=(base + lax.rem(step, team), near), device_id_type=pl.DeviceIdType.MESH
        )
        return carry

    lax.fori_loop(0, crew - team, greet_slab, 0)
    set_borders(fields, layers, rows, depth)
    pl.semaphore_wait(barrier, doms - 1 + crew - team)

    whole_blocks = whole.reshape(layers, rows, depth)
    own_block = pltpu.make_async_copy(logperm.at[slab], whole_blocks.at[pl.ds(slab * width, width)], own_sem.at[0])
    own_block.start()

    def slab_copy(step):
        near = lax.rem(slab + step, slabs)
        return remote(
            logperm.at[near], whole_blocks.at[pl.ds(slab * width, width)],
            slab_send.at[step - 1], slab_recv.at[step - 1], dom, near,
        )

    order = [2, 1, 3]

    for step in order:
        slab_copy(step).start()

    across = lax.rem(slab + 2, slabs)
    beside = slab + 1 - 2 * lax.rem(slab, 2)
    local = []

    def side_copies(which, block, full):
        def at(owner):
            return full.reshape(layers, rows, depth).at[pl.ds(owner * width, width)]

        return [
            remote(block, at(slab), side_send.at[which, 0], side_recv.at[which, 0], dom, across),
            remote(block, at(slab), side_send.at[which, 1], side_recv.at[which, 1], dom, beside),
            remote(at(across), at(across), side_send.at[which, 2], side_recv.at[which, 2], dom, beside),
        ]

    sides = [side_copies(0, source, full_source), side_copies(1, observed, full_observed)]
    for which, (block, full) in enumerate(((source, full_source), (observed, full_observed))):
        copy = pltpu.make_async_copy(block, full.reshape(layers, rows, depth).at[pl.ds(slab * width, width)], own_sem.at[1 + which])
        copy.start()
        local.append(copy)
    sides[0][0].start()
    sides[0][1].start()

    def member_copy(step):
        target = lax.rem(base + team * (1 + step // team), doms) + lax.rem(place + step, team)
        return remote(
            logperm.at[:, lax.rem(target, team)], members.at[pl.ds(dom * particles, particles)],
            member_send.at[step], member_recv.at[step], target, slab,
        )

    def each_member(act, first, last):
        def body(step, carry):
            act(member_copy(step))
            return carry

        lax.fori_loop(first, last, body, 0)

    def start_member(step, carry):
        member_copy(step).start()
        return carry

    lax.fori_loop(0, doms - team, start_member, 0)
    lax.fori_loop(doms - team + 1, doms, start_member, 0)
    own_members = pltpu.make_async_copy(
        logperm.at[:, place], members.at[pl.ds(dom * particles, particles)], own_sem.at[3]
    )
    own_members.start()

    fetch.wait()
    turned = [
        brownian[pl.ds(pl.multiple_of(lax.rem(base + at * team, doms) * particles, 8), crew)]
        for at in range(doms // team)
    ]
    noise[...] = jnp.concatenate(turned, axis=0).T
    own_block.wait()
    for step in order:
        slab_copy(step).wait_recv()
    sides[1][0].start()
    sides[1][1].start()
    coefficients(lambda layer: interleaved(whole, layer, rows), fields)
    sides[0][0].wait_recv()
    sides[0][2].start()
    sides[0][1].wait_recv()
    local[0].wait()
    sides[0][2].wait_recv()

    def forward_observed():
        sides[1][0].wait_recv()
        sides[1][2].start()

    relax(lambda layer: interleaved(full_source, layer, rows), fields[1], fields[2], fields, forward_observed)
    pressure = fields[2]
    sides[1][1].wait_recv()
    local[1].wait()
    sides[1][2].wait_recv()

    def misfit(layer):
        return misfit_weight * (pressure[layer + 1] - interleaved(full_observed, layer, rows))

    relax(misfit, fields[1], fields[3], fields, lambda: None)

    def gradient_copy(step):
        layer, at_dom, at_slab = crew_device(step)
        return remote(
            gradient.at[layer], owned.at[pl.ds(column * rows, rows)],
            gradient_send.at[step - 1], gradient_recv.at[step - 1], at_dom, at_slab,
        )

    def send_gradient(step, carry):
        layer = lax.rem(mine + step, layers)
        gradient[layer] = gradient_layer(layer, fields)
        gradient_copy(step).start()
        return carry

    lax.fori_loop(1, layers, send_gradient, 0, unroll=5)
    owned[pl.ds(column * rows, rows)] = gradient_layer(mine, fields)

    member_rows = members.reshape(ensemble * rows, depth)
    tiles = rows // SUB

    def line(team_at, row):
        first = lax.rem(base + team_at * team, doms) * particles
        return member_rows[pl.ds(first * rows + row, crew, stride=rows)]

    own_members.wait()
    each_member(lambda copy: copy.wait_recv(), doms - team + 1, doms)
    for row in range(rows):
        cells = slice(row * depth, (row + 1) * depth)
        values = line(0, row)
        mean = jnp.sum(values, axis=0, keepdims=True) * (1.0 / crew)
        spread[0:crew, cells] = values - mean
        centre[:, cells] = mean

    def wait_gradient(step, carry):
        gradient_copy(step).wait_recv()
        return carry

    lax.fori_loop(1, crew, wait_gradient, 0)
    piece = min(16, rows)

    def held(first):
        return jnp.concatenate(
            [
                owned[pl.ds((row % tiles) * SUB + row // tiles, crew, stride=rows)]
                for row in range(first, first + piece)
            ],
            axis=1,
        )

    for team_at in range(doms // team):
        at = slice(team_at * crew, (team_at + 1) * crew)
        if team_at > 0:
            each_member(lambda copy: copy.wait_recv(), (team_at - 1) * team, team_at * team)
            for row in range(rows):
                cells = slice(row * depth, (row + 1) * depth)
                spread[at, cells] = line(team_at, row) - centre[:, cells]
        gram = jnp.zeros((crew, crew), jnp.float32)
        for first in range(0, rows, piece):
            gram = gram + product(held(first), spread[at, first * depth : (first + piece) * depth], 1)
        parts[mine, :, at] = gram

    def part_copy(step):
        _, at_dom, at_slab = crew_device(step)
        return remote(
            parts.at[mine], parts.at[mine], part_send.at[step - 1], part_recv.at[step - 1], at_dom, at_slab
        )

    def start_part(step, carry):
        part_copy(step).start()
        return carry

    def wait_part(step, carry):
        part_copy(step).wait_recv()
        return carry

    lax.fori_loop(1, crew, start_part, 0)
    lax.fori_loop(1, crew, wait_part, 0)
    gram = jnp.sum(parts[...], axis=0)
    gram = gram - jnp.sum(gram, axis=1, keepdims=True) * (1.0 / ensemble)
    step_size = ensemble / (4.0 * (layers * rows * depth + 1))
    first_column = pl.multiple_of(base * particles, 8)
    mixing = -(step_size / ensemble) * gram + math.sqrt(2.0 * step_size / ensemble) * noise[
        pl.ds(first_column, crew)
    ]
    mixing = mixing - (jnp.sum(mixing, axis=1, keepdims=True) + 0.25) * (1.0 / ensemble)
    moved_block = moved.reshape(crew, rows, depth)

    def result_part(to, first):
        return (
            moved_block.at[pl.ds(to * particles, particles), pl.ds(first, part)],
            moved_out.at[:, pl.ds(place * rows + first, part)],
        )

    def result_copy(step, first):
        to = lax.rem(place + step, team)
        at = first // part
        return remote(
            *result_part(to, first), result_send.at[at, step - 1], result_recv.at[at, step - 1],
            base + to, slab,
        )

    part = rows // 2
    own_results = []
    for first in range(0, rows, part):
        cells = slice(first * depth, (first + part) * depth)
        result = spread[0:crew, cells] * 1.25 + centre[:, cells] + product(mixing, spread[:, cells], 0)
        for row in range(part):
            moved[pl.ds(first + row, crew, stride=rows)] = result[:, row * depth : (row + 1) * depth]
        for step in range(1, team):
            result_copy(step, first).start()
        copy = pltpu.make_async_copy(*result_part(place, first), own_sem.at[6 + first // part])
        copy.start()
        own_results.append(copy)

    for step in order:
        slab_copy(step).wait_send()
    for which in range(2):
        for copy in sides[which]:
            copy.wait_send()

    def sent_crew(step, carry):
        gradient_copy(step).wait_send()
        part_copy(step).wait_send()
        return carry

    each_member(lambda copy: copy.wait_send(), 0, doms - team)
    each_member(lambda copy: copy.wait_send(), doms - team + 1, doms)
    lax.fori_loop(1, crew, sent_crew, 0)
    for copy in own_results:
        copy.wait()
    for first in range(0, rows, part):
        for step in range(1, team):
            result_copy(step, first).wait()


def hand_over(moved, out, sems):
    copies = [
        pltpu.make_async_copy(moved.at[particle, layer], out.at[particle, layer], sems.at[particle, layer])
        for particle in range(moved.shape[0])
        for layer in range(moved.shape[1])
    ]
    for copy in copies:
        copy.start()
    for copy in copies:
        copy.wait()


def on_device(logperm, source, observed, brownian):
    particles, width, rows, depth = logperm.shape
    slabs, doms = lax.axis_size("slab"), lax.axis_size("dom")
    assert particles == slabs == 4 and doms % width == 0
    layers, crew, ensemble = width * slabs, width * slabs, doms * particles
    f32 = jnp.float32
    dma = pltpu.SemaphoreType.DMA
    scratch = [
        pltpu.VMEM((ensemble, ensemble), f32),
        pltpu.VMEM((layers * rows, depth), f32),
        pltpu.VMEM((layers * rows, depth), f32),
        pltpu.VMEM((layers * rows, depth), f32),
        pltpu.VMEM((layers, rows, depth), f32),
        pltpu.VMEM((ensemble, rows, depth), f32),
        pltpu.VMEM((ensemble, rows * depth), f32),
        pltpu.VMEM((1, rows * depth), f32),
        pltpu.VMEM((crew * rows, depth), f32),
        pltpu.VMEM((crew * rows, depth), f32),
        pltpu.VMEM((crew, crew, ensemble), f32),
        pltpu.VMEM((ensemble, ensemble), f32),
        dma((slabs - 1,)), dma((slabs - 1,)),
        dma((2, 3)), dma((2, 3)),
        dma((doms,)), dma((doms,)),
        dma((8,)),
        dma((crew - 1,)), dma((crew - 1,)),
        dma((crew - 1,)), dma((crew - 1,)),
        dma((2, width - 1)), dma((2, width - 1)),
        *scratch_fields(layers, rows, depth),
    ]
    far = pl.BlockSpec(memory_space=pltpu.HBM)
    moved = pl.pallas_call(
        fused_kernel,
        out_shape=jax.ShapeDtypeStruct((particles, width * rows, depth), f32),
        in_specs=[far] * 4,
        out_specs=far,
        scratch_shapes=scratch,
        compiler_params=pltpu.CompilerParams(
            collective_id=0, has_side_effects=True, vmem_limit_bytes=VMEM_BYTES
        ),
        cost_estimate=pl.CostEstimate(
            flops=logperm.size * 300, bytes_accessed=logperm.size * 16, transcendentals=logperm.size
        ),
        name="langevin",
    )(logperm, source, observed, brownian)
    return pl.pallas_call(
        hand_over,
        out_shape=jax.ShapeDtypeStruct(logperm.shape, f32),
        in_specs=[far],
        out_specs=far,
        scratch_shapes=[dma((particles, width))],
        name="hand_over",
    )(moved.reshape(logperm.shape))


def solution(mesh):
    return jax.shard_map(
        on_device,
        mesh=mesh,
        in_specs=(P("dom", "slab", None, None), P("slab", None, None), P("slab", None, None), P()),
        out_specs=P("dom", "slab", None, None),
        check_vma=False,
    )
```
